512 devices in a mesh: ctx: 64 (over z, y_lo, core), tp: 8 (over y_hi, x).
Axes of the slice: x: 4, y: 8 (y_hi: 2, y_lo: 4; y = y_hi * 4 + y_lo), z: 8, core: 2. Of those that a mesh axis runs over, the one named last changes fastest.
Arguments:
- queries: bfloat16 [512, 65536], P('tp', 'ctx'), may hold values from -6 to 6
- keys: bfloat16 [512, 65536], P('tp', 'ctx'), may hold values from -6 to 6
- values: bfloat16 [512, 65536], P('tp', 'ctx'), may hold values from -6 to 6
- grad_out: bfloat16 [512, 65536], P('tp', 'ctx'), may hold values from -6 to 6
- residues: float32 [512, 16], P('tp'), may hold values from -1.5 to 1.5
- decay_rate: float32 [512, 16], P('tp'), may hold values from 7.6293946e-07 to 0.033
- skip_gain: float32 [512], P('tp'), may hold values from -4 to 4
Outputs:
- grad_queries: bfloat16 [512, 65536], P('tp', 'ctx')
- grad_keys: bfloat16 [512, 65536], P('tp', 'ctx')
- grad_values: bfloat16 [512, 65536], P('tp', 'ctx')
- grad_residues: float32 [512, 16], P('tp')
- grad_skip: float32 [512], P('tp')
The draws below stay inside these ranges and needn't reach their ends.
All inputs are finite; a program needn't handle non-finite values.
Results may differ from the reference program's by a relative error of at most 0.0035.
Values may be sent and summed in bfloat16 or wider, within the bound.
No kernel may reach another device: no remote copies, remote signals or barrier semaphores. Data moves between devices by JAX's collectives and lax.ppermute only.
A program may use at most 64 MiB of HBM per device.

```python
import math
import jax
import jax.numpy as jnp
from jax import lax

MODES = 16
CH = 512
TOKENS = 65536


def block_scale(own_key, shape, cuts, smallest, largest):
    level = 1.0
    for dim, shards_of in cuts:
        heights = jax.random.uniform(jax.random.fold_in(jax.random.fold_in(own_key, 6), dim), (shards_of,), jnp.float32, smallest / len(cuts), largest / len(cuts))
        level = level * jnp.repeat(jnp.exp(heights), shape[dim] // shards_of).reshape((-1,) + (1,) * (len(shape) - 1 - dim))
    return level


def centred(stream_key, shape, deviation, reach, cuts=(), held_as=jnp.bfloat16):
    entries = jax.random.normal(stream_key, shape, jnp.float32) * deviation
    if len(cuts) > 0:
        entries = block_scale(stream_key, shape, cuts, -0.22, 0.18) * entries
    return jnp.clip(entries, min=-reach, max=reach).astype(held_as)


def setup_inputs(seed: int = 0) -> dict:
    arg_keys = jax.random.split(jax.random.key(seed), 8)
    return {
        "queries": centred(arg_keys[0], (CH, TOKENS), 1.0, 6.0, ((0, 8), (1, 64))),
        "keys": centred(arg_keys[1], (CH, TOKENS), 1.0, 6.0, ((0, 8), (1, 64))),
        "values": centred(arg_keys[2], (CH, TOKENS), 1.0, 6.0, ((0, 8), (1, 64))),
        "grad_out": centred(arg_keys[3], (CH, TOKENS), 1.0, 6.0, ((0, 8), (1, 64))),
        "residues": centred(arg_keys[4], (CH, MODES), MODES ** -0.5, 1.5, ((0, 8),), jnp.float32),
        "decay_rate": jnp.clip(jnp.exp(math.log(0.033) - 10.674839 * jax.random.uniform(arg_keys[5], (CH, MODES), jnp.float32) ** block_scale(arg_keys[5], (CH, MODES), ((0, 8),), -0.2, 0.2)), 7.629394644936838e-07, 0.033),
        "skip_gain": centred(arg_keys[6], (CH,), 1.0, 4.0, ((0, 8),), jnp.float32),
    }


def channel_group(pieces):
    units, signal, weight, factor, skip = pieces
    width = units.shape[0]
    zeros = jnp.zeros((width, weight.shape[1]), jnp.float32)

    def forward(carry, columns):
        state, total = carry
        unit_col, grad_col = columns
        state = factor * state + unit_col[:, None]
        mixed_col = lax.optimization_barrier(jnp.sum(weight * state, axis=1)) + skip * unit_col
        total = total + grad_col[:, None] * state
        return ((state, total), mixed_col)
    (final_state, totals), mixed = lax.scan(forward, (zeros, zeros), (units.T, signal.T), unroll=8)

    def backward(state, grad_col):
        state = factor * state + grad_col[:, None]
        back_col = lax.optimization_barrier(jnp.sum(weight * state, axis=1)) + skip * grad_col
        return (state, back_col)
    final_back, back = lax.scan(backward, zeros, signal.T, reverse=True, unroll=8)
    direct = lax.optimization_barrier(jnp.sum(signal * units, axis=1))
    return (mixed.T, back.T, totals, direct)

def reference(queries, keys, values, grad_out, residues, decay_rate, skip_gain):
    gain = jnp.sqrt(-jnp.expm1(-2.0 * decay_rate))
    weight = residues * gain
    factor = jnp.exp(-decay_rate)
    units = keys.astype(jnp.float32) * values.astype(jnp.float32)
    signal = grad_out.astype(jnp.float32) * queries.astype(jnp.float32)
    group_width = 64
    groups = units.shape[0] // group_width
    length = units.shape[1]

    def split(array):
        return array.reshape((groups, group_width) + array.shape[1:])
    mixed, back, totals, direct = lax.map(channel_group, (split(units), split(signal), split(weight), split(factor), split(skip_gain)))
    mixed = mixed.reshape(-1, length)
    back = back.reshape(-1, length)
    totals = totals.reshape(-1, weight.shape[1])
    direct = direct.reshape(-1)
    grad_queries = (grad_out.astype(jnp.float32) * mixed).astype(jnp.bfloat16)
    grad_keys = (back * values.astype(jnp.float32)).astype(jnp.bfloat16)
    grad_values = (back * keys.astype(jnp.float32)).astype(jnp.bfloat16)
    norm = math.sqrt(TOKENS)
    grad_residues = gain * totals / norm
    grad_skip = direct / norm
    return (grad_queries, grad_keys, grad_values, grad_residues, grad_skip)
```

```python
import functools
import math

import jax
import jax.numpy as jnp
from jax import lax
from jax.experimental import pallas as pl
from jax.experimental.pallas import tpu as pltpu
from jax.sharding import PartitionSpec as P

MODES = 16
LANES = 128
SUB = 8
HALF = 64
STEPS = 64
CHUNKS = 16
LOCAL = STEPS * CHUNKS
GROUP = 8
F32 = jnp.float32


def iota(shape, dim):
    return lax.broadcasted_iota(jnp.int32, shape, dim)


def mode_rows(table):
    wide = jnp.concatenate([table, jnp.zeros((HALF, LANES - MODES), F32)], axis=1)
    turned = jnp.concatenate([wide, wide], axis=0).T
    return turned[:MODES]


def to_steps(x, out_ref):
    for p in range(4):
        low = x[:, p * LANES : (p + 1) * LANES]
        high = x[:, (p + 4) * LANES : (p + 5) * LANES]
        out_ref[p * LANES : (p + 1) * LANES, :] = jnp.concatenate([low, high], axis=0).T


def step_rows(step):
    return pl.ds(step, SUB, stride=STEPS)


def summary_kernel(
    q_ref, k_ref, v_ref, g_ref, rate_ref, ut_ref, st_ref, sf_ref, sb_ref, msg_ref
):
    to_steps(k_ref[...].astype(F32) * v_ref[...].astype(F32), ut_ref)
    to_steps(g_ref[...].astype(F32) * q_ref[...].astype(F32), st_ref)
    rates = mode_rows(rate_ref[...])
    row = iota((SUB, LANES), 0)
    upper = iota((SUB, LANES), 1) >= HALF
    row_f = row.astype(F32)
    zero = jnp.zeros((SUB, LANES), F32)
    ends, adjoints, totals = [], [], []
    for half in range(2):
        modes = range(half * 8, half * 8 + 8)
        wide = [jnp.broadcast_to(rates[m : m + 1], (SUB, LANES)) for m in modes]
        factor = [jnp.exp(-r) for r in wide]

        def body(i, carry):
            state, total, back, direct = carry
            u = ut_ref[step_rows(i), :]
            s = st_ref[step_rows(i), :]
            sb = st_ref[step_rows(STEPS - 1 - i), :]
            state = [f * x + u for f, x in zip(factor, state)]
            total = [t + s * x for t, x in zip(total, state)]
            back = [f * x + sb for f, x in zip(factor, back)]
            return state, total, back, direct + s * u

        state, total, back, direct = lax.fori_loop(
            0, STEPS, body, ([zero] * 8, [zero] * 8, [zero] * 8, zero), unroll=8
        )
        for n, m in enumerate(modes):
            r = wide[n]
            decay = [jnp.exp(-(STEPS * d) * r) for d in (1, 2, 4)]
            half_decay = jnp.exp(-(STEPS * SUB) * r)
            scan = state[n]
            scan_b = back[n]
            for d, w in zip((1, 2, 4), decay):
                scan = scan + jnp.where(row >= d, w * pltpu.roll(scan, d, 0), 0.0)
                scan_b = scan_b + jnp.where(row < SUB - d, w * pltpu.roll(scan_b, SUB - d, 0), 0.0)
            last = jnp.broadcast_to(scan[SUB - 1 : SUB], (SUB, LANES))
            first = jnp.broadcast_to(scan_b[0:1], (SUB, LANES))
            last_other = pltpu.roll(last, HALF, 1)
            first_other = pltpu.roll(first, HALF, 1)
            start = jnp.where(row >= 1, pltpu.roll(scan, 1, 0), 0.0)
            start = start + jnp.where(upper, jnp.exp(-STEPS * row_f * r) * last_other, 0.0)
            start_b = jnp.where(row < SUB - 1, pltpu.roll(scan_b, SUB - 1, 0), 0.0)
            start_b = start_b + jnp.where(
                upper, 0.0, jnp.exp(-STEPS * (SUB - 1 - row_f) * r) * first_other
            )
            sf_ref[m] = start
            sb_ref[m] = start_b
            ends.append((last + half_decay * last_other)[0:1])
            adjoints.append((first + half_decay * first_other)[0:1])
            totals.append(
                jnp.sum(total[n] + start * factor[n] * back[n], axis=0, keepdims=True)
            )
    ends = jnp.concatenate(ends, axis=0)
    adjoints = jnp.concatenate(adjoints, axis=0)
    totals = jnp.concatenate(totals, axis=0)
    direct = jnp.broadcast_to(jnp.sum(direct, axis=0, keepdims=True), (MODES, LANES))
    totals = totals + pltpu.roll(totals, HALF, 1)
    direct = direct + pltpu.roll(direct, HALF, 1)
    lanes_up = iota((MODES, LANES), 1) >= HALF
    pair = jnp.where(lanes_up, ends, adjoints)
    sums = jnp.where(lanes_up, direct, totals)
    for j in range(GROUP):
        msg_ref[j, 0:MODES] = pair
        msg_ref[j, MODES : 2 * MODES] = sums


def combine(got_ref, rates, span, place):
    lanes_up = iota((MODES, LANES), 1) >= HALF
    rho = jnp.exp(-float(span) * rates)
    factor = jnp.exp(-rates)
    zero = jnp.zeros((MODES, LANES), F32)
    pairs = [got_ref[k, 0:MODES] for k in range(GROUP)]
    fwd, bwd = zero, zero
    enter_f, enter_b = zero, zero
    cross = zero
    sums = zero
    for k in range(GROUP):
        enter_f = jnp.where(place == k, fwd, enter_f)
        cross = cross + fwd * factor * pltpu.roll(pairs[k], HALF, 1)
        fwd = rho * fwd + pairs[k]
        sums = sums + got_ref[k, MODES : 2 * MODES]
    for k in reversed(range(GROUP)):
        enter_b = jnp.where(place == k, bwd, enter_b)
        bwd = rho * bwd + pairs[k]
    entering = jnp.where(lanes_up, enter_f, enter_b)
    joint = jnp.where(lanes_up, fwd, bwd)
    sums = sums + jnp.where(lanes_up, 0.0, pltpu.roll(cross, HALF, 1))
    return joint, sums, entering


def middle_kernel(place_ref, got_ref, rate_ref, msg_ref, enter_ref):
    rates = mode_rows(rate_ref[...])
    joint, sums, entering = combine(got_ref, rates, LOCAL, place_ref[0])
    enter_ref[...] = entering
    for j in range(GROUP):
        msg_ref[j, 0:MODES] = joint
        msg_ref[j, MODES : 2 * MODES] = sums


def final_kernel(
    place_ref,
    got_ref,
    enter_ref,
    sf_ref,
    sb_ref,
    ut_ref,
    st_ref,
    k_ref,
    v_ref,
    g_ref,
    rate_ref,
    weight_ref,
    gain_ref,
    skip_ref,
    gq_ref,
    gk_ref,
    gv_ref,
    gr_ref,
    gs_ref,
    mixed_ref,
    back_ref,
):
    rates = mode_rows(rate_ref[...])
    weights = mode_rows(weight_ref[...])
    joint, sums, outer = combine(got_ref, rates, LOCAL * GROUP, place_ref[1])
    lanes_up = iota((MODES, LANES), 1) >= HALF
    inner_place = place_ref[0]
    ahead = jnp.where(lanes_up, inner_place, GROUP - 1 - inner_place).astype(F32)
    entering = enter_ref[...] + jnp.exp(-(LOCAL * ahead) * rates) * outer
    turned = pltpu.roll(entering, HALF, 1)
    enter_f = jnp.where(lanes_up, entering, turned)
    enter_b = jnp.where(lanes_up, turned, entering)

    norm = 1.0 / math.sqrt(65536)
    tall = jnp.concatenate([sums, jnp.zeros((LANES - MODES, LANES), F32)], axis=0).T
    gr_ref[...] = gain_ref[...] * tall[:HALF, :MODES] * norm
    gs_ref[...] = sums[0:1, HALF:] * norm

    row = iota((SUB, LANES), 0)
    upper = iota((SUB, LANES), 1) >= HALF
    chunk = (row + jnp.where(upper, SUB, 0)).astype(F32)
    wide = [jnp.broadcast_to(rates[m : m + 1], (SUB, LANES)) for m in range(MODES)]
    factor = [jnp.exp(-r) for r in wide]
    weight = [jnp.broadcast_to(weights[m : m + 1], (SUB, LANES)) for m in range(MODES)]
    skip = jnp.broadcast_to(jnp.concatenate([skip_ref[...], skip_ref[...]], axis=1), (SUB, LANES))

    def added(terms):
        while len(terms) > 1:
            terms = [a + b for a, b in zip(terms[::2], terms[1::2])]
        return terms[0]

    def run(src_ref, dst_ref, start, flip):
        def body(i, state):
            rows = step_rows(STEPS - 1 - i if flip else i)
            x = src_ref[rows, :]
            state = [f * z + x for f, z in zip(factor, state)]
            dst_ref[rows, :] = added([w * z for w, z in zip(weight, state)]) + skip * x
            return state

        lax.fori_loop(0, STEPS, body, start, unroll=8)

    def lift(m, rows):
        return jnp.broadcast_to(rows[m : m + 1], (SUB, LANES))

    start_f = [
        sf_ref[m] + jnp.exp(-(STEPS * chunk) * wide[m]) * lift(m, enter_f) for m in range(MODES)
    ]
    run(ut_ref, mixed_ref, start_f, False)
    start_b = [
        sb_ref[m] + jnp.exp(-(STEPS * (CHUNKS - 1 - chunk)) * wide[m]) * lift(m, enter_b)
        for m in range(MODES)
    ]
    run(st_ref, back_ref, start_b, True)

    for p in range(4):
        rows = slice(p * LANES, (p + 1) * LANES)
        mixed = mixed_ref[rows, :].T
        back = back_ref[rows, :].T
        for b in range(2):
            cols = slice((p + 4 * b) * LANES, (p + 4 * b + 1) * LANES)
            chans = slice(b * HALF, (b + 1) * HALF)
            gq_ref[:, cols] = (g_ref[:, cols].astype(F32) * mixed[chans]).astype(jnp.bfloat16)
            gk_ref[:, cols] = (v_ref[:, cols].astype(F32) * back[chans]).astype(jnp.bfloat16)
            gv_ref[:, cols] = (k_ref[:, cols].astype(F32) * back[chans]).astype(jnp.bfloat16)


VMEM = pl.BlockSpec(memory_space=pltpu.VMEM)
SMEM = pl.BlockSpec(memory_space=pltpu.SMEM)
PARAMS = pltpu.CompilerParams(vmem_limit_bytes=32 * 1024 * 1024)
MESSAGE = jax.ShapeDtypeStruct((GROUP, 2 * MODES, LANES), F32)
STATES = jax.ShapeDtypeStruct((MODES, SUB, LANES), F32)
STEPPED = jax.ShapeDtypeStruct((STEPS * SUB, LANES), F32)


def shards(queries, keys, values, grad_out, residues, decay_rate, skip_gain):
    gain = jnp.sqrt(-jnp.expm1(-2.0 * decay_rate))
    weight = residues * gain
    me = lax.axis_index("ctx")
    place = jnp.stack([me % GROUP, me // GROUP]).astype(jnp.int32)
    near = [[z * GROUP + k for k in range(GROUP)] for z in range(GROUP)]
    far = [[z * GROUP + k for z in range(GROUP)] for k in range(GROUP)]

    ut, st, sf, sb, msg = pl.pallas_call(
        summary_kernel,
        out_shape=(STEPPED, STEPPED, STATES, STATES, MESSAGE),
        in_specs=[VMEM] * 5,
        out_specs=(VMEM,) * 5,
        compiler_params=PARAMS,
        name="summary",
    )(queries, keys, values, grad_out, decay_rate)
    got = lax.all_to_all(msg, "ctx", 0, 0, axis_index_groups=near)
    msg, enter = pl.pallas_call(
        middle_kernel,
        out_shape=(MESSAGE, jax.ShapeDtypeStruct((MODES, LANES), F32)),
        in_specs=[SMEM, VMEM, VMEM],
        out_specs=(VMEM,) * 2,
        compiler_params=PARAMS,
        name="middle",
    )(place, got, decay_rate)
    got = lax.all_to_all(msg, "ctx", 0, 0, axis_index_groups=far)
    wide = jax.ShapeDtypeStruct(queries.shape, jnp.bfloat16)
    grad_q, grad_k, grad_v, grad_res, grad_skip = pl.pallas_call(
        final_kernel,
        out_shape=(
            wide,
            wide,
            wide,
            jax.ShapeDtypeStruct((HALF, MODES), F32),
            jax.ShapeDtypeStruct((1, HALF), F32),
        ),
        in_specs=[SMEM] + [VMEM] * 13,
        out_specs=(VMEM,) * 5,
        scratch_shapes=[pltpu.VMEM((STEPS * SUB, LANES), F32)] * 2,
        compiler_params=PARAMS,
        name="final",
    )(
        place,
        got,
        enter,
        sf,
        sb,
        ut,
        st,
        keys,
        values,
        grad_out,
        decay_rate,
        weight,
        gain,
        skip_gain.reshape(1, HALF),
    )
    return (grad_q, grad_k, grad_v, grad_res, grad_skip.reshape(HALF))


def solution(mesh):
    in_specs = (
        P("tp", "ctx"),
        P("tp", "ctx"),
        P("tp", "ctx"),
        P("tp", "ctx"),
        P("tp", None),
        P("tp", None),
        P("tp"),
    )
    out_specs = (P("tp", "ctx"), P("tp", "ctx"), P("tp", "ctx"), P("tp", None), P("tp"))
    return jax.shard_map(shards, mesh=mesh, in_specs=in_specs, out_specs=out_specs, check_vma=False)
```

```python
import math

import jax
import jax.numpy as jnp
from jax import lax
from jax.experimental import pallas as pl
from jax.experimental.pallas import tpu as pltpu
from jax.sharding import PartitionSpec as P

MODES = 16
LANES = 128
SUB = 8
HALF = 64
STEPS = 64
PITCH = STEPS + 1
CHUNKS = 16
LOCAL = STEPS * CHUNKS
GROUP = 8
F32 = jnp.float32


def iota(shape, dim):
    return lax.broadcasted_iota(jnp.int32, shape, dim)


def twice(rows):
    return jnp.concatenate([rows, rows], axis=1)


def lift(rows, m):
    return jnp.broadcast_to(rows[m : m + 1], (SUB, LANES))


def to_steps(x, out_ref):
    for p in range(4):
        low = x[:, p * LANES : (p + 1) * LANES]
        high = x[:, (p + 4) * LANES : (p + 5) * LANES]
        turned = jnp.concatenate([low, high], axis=0).T
        for q in range(2):
            first = (2 * p + q) * PITCH
            out_ref[first : first + STEPS, :] = turned[q * STEPS : (q + 1) * STEPS]


def from_steps(ref, p):
    first = 2 * p * PITCH
    parts = [ref[first : first + STEPS, :], ref[first + PITCH : first + PITCH + STEPS, :]]
    return jnp.concatenate(parts, axis=0).T


def step_rows(step):
    return pl.ds(step, SUB, stride=PITCH)


def summary_kernel(
    q_any, k_any, v_any, g_any, rate_any,
    ut_any, st_any, sf_any, xb_any, msg_any,
    q_ref, k_ref, v_ref, g_ref, rate_ref, ut_ref, st_ref, sf_ref, xb_ref, msg_ref,
    row_ref, decay_ref, in_sems, out_sems, msg_sems,
):
    pairs = ((rate_any, rate_ref), (k_any, k_ref), (v_any, v_ref), (g_any, g_ref), (q_any, q_ref))
    copies = [pltpu.make_async_copy(a, b, in_sems.at[n]) for n, (a, b) in enumerate(pairs)]
    for copy in copies:
        copy.start()

    copies[0].wait()
    rates = twice(rate_ref[...])
    row_ref[0] = rates
    row_ref[1] = jnp.exp(-rates)
    row_ref[2] = jnp.exp(-float(STEPS * SUB) * rates)
    row = iota((SUB, LANES), 0)
    upper = iota((SUB, LANES), 1) >= HALF
    row_f = row.astype(F32)
    chunk = jnp.where(upper, row_f + SUB, row_f)
    for m in range(MODES):
        r = row_ref[0, m : m + 1, :]
        for n, d in enumerate((1, 2, 4)):
            decay_ref[m, n] = jnp.where(row >= d, jnp.exp(-float(STEPS * d) * r), 0.0)
        decay_ref[m, 3] = jnp.where(upper, jnp.exp(-(STEPS * row_f) * r), 0.0)
        decay_ref[m, 4] = jnp.exp(-(STEPS * chunk) * r)

    copies[1].wait()
    copies[2].wait()
    to_steps(k_ref[...].astype(F32) * v_ref[...].astype(F32), ut_ref)
    copy_u = pltpu.make_async_copy(ut_ref, ut_any, out_sems.at[0])
    copy_u.start()
    copies[3].wait()
    copies[4].wait()
    to_steps(g_ref[...].astype(F32) * q_ref[...].astype(F32), st_ref)
    copy_s = pltpu.make_async_copy(st_ref, st_any, out_sems.at[1])
    copy_s.start()

    zero = jnp.zeros((SUB, LANES), F32)
    ends, adjoints, totals = [], [], []
    for half in range(2):
        modes = range(half * 8, half * 8 + 8)
        factor = [jnp.broadcast_to(row_ref[1, m : m + 1, :], (SUB, LANES)) for m in modes]

        def body(i, carry):
            state, total, back, direct = carry
            u = ut_ref[step_rows(i), :]
            s = st_ref[step_rows(i), :]
            sb = st_ref[step_rows(STEPS - 1 - i), :]
            state = [f * x + u for f, x in zip(factor, state)]
            total = [t + s * x for t, x in zip(total, state)]
            back = [f * x + sb for f, x in zip(factor, back)]
            if half == 0:
                direct = direct + s * u
            return state, total, back, direct

        if half == 0:
            direct = zero
        state, total, back, direct = lax.fori_loop(
            0, STEPS, body, ([zero] * 8, [zero] * 8, [zero] * 8, direct), unroll=8
        )
        for n, m in enumerate(modes):
            scan = state[n]
            for j, d in enumerate((1, 2, 4)):
                scan = scan + decay_ref[m, j] * pltpu.roll(scan, d, 0)
            last = scan[SUB - 1 : SUB]
            last_other = pltpu.roll(last, HALF, 1)
            start = jnp.where(row >= 1, pltpu.roll(scan, 1, 0), 0.0)
            start = start + decay_ref[m, 3] * last_other
            sf_ref[m] = start
            xb_ref[m] = back[n]
            ends.append(last + row_ref[2, m : m + 1, :] * last_other)
            adjoints.append(jnp.sum(decay_ref[m, 4] * back[n], axis=0, keepdims=True))
            totals.append(
                jnp.sum(total[n] + start * factor[n] * back[n], axis=0, keepdims=True)
            )
    copy_sf = pltpu.make_async_copy(sf_ref, sf_any, out_sems.at[2])
    copy_sf.start()
    copy_xb = pltpu.make_async_copy(xb_ref, xb_any, out_sems.at[3])
    copy_xb.start()
    ends = jnp.concatenate(ends, axis=0)
    adjoints = jnp.concatenate(adjoints, axis=0)
    totals = jnp.concatenate(totals, axis=0)
    direct = jnp.broadcast_to(jnp.sum(direct, axis=0, keepdims=True), (MODES, LANES))
    adjoints = adjoints + pltpu.roll(adjoints, HALF, 1)
    totals = totals + pltpu.roll(totals, HALF, 1)
    direct = direct + pltpu.roll(direct, HALF, 1)
    lanes_up = iota((MODES, LANES), 1) >= HALF
    msg_ref[0:MODES] = jnp.where(lanes_up, ends, adjoints)
    msg_ref[MODES : 2 * MODES] = jnp.where(lanes_up, direct, totals)
    sends = [
        pltpu.make_async_copy(msg_ref, msg_any.at[j], msg_sems.at[j]) for j in range(GROUP)
    ]
    for copy in sends:
        copy.start()
    for copy in [copy_u, copy_s, copy_sf, copy_xb] + sends:
        copy.wait()


def local_kernel(
    place_ref, ut_ref, st_ref, sf_ref, xb_ref, rate_ref, weight_ref, gain_ref, skip_ref,
    mixed_ref, back_ref, zf_ref, zb_ref, table_ref, near_ref, far_ref,
):
    rates = twice(rate_ref[...])
    weights = twice(weight_ref[...])
    skip_row = skip_ref[...]
    skip = jnp.broadcast_to(jnp.concatenate([skip_row, skip_row], axis=1), (SUB, LANES))
    wide = [lift(rates, m) for m in range(MODES)]
    factor = [jnp.exp(-r) for r in wide]
    weight = [lift(weights, m) for m in range(MODES)]

    def added(terms):
        while len(terms) > 1:
            terms = [a + b for a, b in zip(terms[::2], terms[1::2])]
        return terms[0]

    def run(src_ref, dst_ref, start, flip):
        def body(i, state):
            rows = step_rows(STEPS - 1 - i if flip else i)
            x = src_ref[rows, :]
            state = [f * z + x for f, z in zip(factor, state)]
            dst_ref[rows, :] = added([w * z for w, z in zip(weight, state)]) + skip * x
            return state

        lax.fori_loop(0, STEPS, body, start, unroll=8)

    row = iota((SUB, LANES), 0)
    upper = iota((SUB, LANES), 1) >= HALF
    run(ut_ref, mixed_ref, [sf_ref[m] for m in range(MODES)], False)
    start_b = []
    for m in range(MODES):
        scan = xb_ref[m]
        for d in (1, 2, 4):
            decay = jnp.where(row < SUB - d, jnp.exp(-float(STEPS * d) * wide[m]), 0.0)
            scan = scan + decay * pltpu.roll(scan, SUB - d, 0)
        first_other = pltpu.roll(lift(scan, 0), HALF, 1)
        start = jnp.where(row < SUB - 1, pltpu.roll(scan, SUB - 1, 0), 0.0)
        decay = jnp.exp(-(STEPS * (SUB - 1 - row).astype(F32)) * wide[m])
        start_b.append(start + jnp.where(upper, 0.0, decay * first_other))
    run(st_ref, back_ref, start_b, True)

    chunk = (row + jnp.where(upper, SUB, 0)).astype(F32)
    for m in range(MODES):
        zf_ref[m] = weight[m] * jnp.exp(-(STEPS * chunk + 1.0) * wide[m])
        zb_ref[m] = weight[m] * jnp.exp(-(STEPS * (CHUNKS - 1 - chunk) + 1.0) * wide[m])
    lanes_up = iota((MODES, LANES), 1) >= HALF
    place = place_ref[0]
    ahead = jnp.where(lanes_up, place, GROUP - 1 - place).astype(F32)
    for k in range(GROUP):
        near_ref[k] = jnp.broadcast_to((place == k).astype(F32), (MODES, LANES))
        far_ref[k] = jnp.broadcast_to((place_ref[1] == k).astype(F32), (MODES, LANES))
    table_ref[0] = jnp.exp(-rates)
    table_ref[1] = jnp.exp(-float(LOCAL) * rates)
    table_ref[2] = jnp.exp(-float(LOCAL * GROUP) * rates)
    table_ref[3] = jnp.exp(-(LOCAL * ahead) * rates)
    norm = 1.0 / math.sqrt(65536)
    table_ref[4] = jnp.where(lanes_up, norm, twice(gain_ref[...]) * norm)


def combine(got_ref, factor, rho, chosen_ref):
    lanes_up = iota((MODES, LANES), 1) >= HALF
    zero = jnp.zeros((MODES, LANES), F32)
    pairs = [got_ref[k, 0:MODES] for k in range(GROUP)]
    fwd, bwd = zero, zero
    enter_f, enter_b = zero, zero
    cross = zero
    sums = zero
    for k in range(GROUP):
        enter_f = enter_f + chosen_ref[k] * fwd
        cross = cross + fwd * pltpu.roll(pairs[k], HALF, 1)
        fwd = rho * fwd + pairs[k]
        sums = sums + got_ref[k, MODES : 2 * MODES]
    for k in reversed(range(GROUP)):
        enter_b = enter_b + chosen_ref[k] * bwd
        bwd = rho * bwd + pairs[k]
    entering = jnp.where(lanes_up, enter_f, enter_b)
    joint = jnp.where(lanes_up, fwd, bwd)
    sums = sums + jnp.where(lanes_up, 0.0, pltpu.roll(factor * cross, HALF, 1))
    return joint, sums, entering


def middle_kernel(got_ref, table_ref, near_ref, msg_ref, enter_ref):
    joint, sums, entering = combine(got_ref, table_ref[0], table_ref[1], near_ref)
    enter_ref[...] = entering
    for j in range(GROUP):
        msg_ref[j, 0:MODES] = joint
        msg_ref[j, MODES : 2 * MODES] = sums


def final_kernel(
    got_ref, enter_ref, table_ref, far_ref, zf_ref, zb_ref, mixed_ref, back_ref,
    k_ref, v_ref, g_ref,
    gq_any, gk_any, gv_any, gr_ref, gs_ref,
    gq_ref, gk_ref, gv_ref, fwd_ref, bwd_ref, sems,
):
    factors = table_ref[0]
    joint, sums, outer = combine(got_ref, factors, table_ref[2], far_ref)
    lanes_up = iota((MODES, LANES), 1) >= HALF
    entering = enter_ref[...] + table_ref[3] * outer
    turned = pltpu.roll(entering, HALF, 1)
    enter_f = jnp.where(lanes_up, entering, turned)
    enter_b = jnp.where(lanes_up, turned, entering)
    scaled = sums * table_ref[4]
    gr_ref[...] = scaled[:, :HALF]
    gs_ref[...] = scaled[0:1, HALF:]

    factor = [lift(factors, m) for m in range(MODES)]

    def added(terms):
        while len(terms) > 1:
            terms = [a + b for a, b in zip(terms[::2], terms[1::2])]
        return terms[0]

    def run(src_ref, dst_ref, start, flip):
        def body(i, z):
            rows = step_rows(STEPS - 1 - i if flip else i)
            dst_ref[rows, :] = src_ref[rows, :] + added(z)
            return [f * x for f, x in zip(factor, z)]

        lax.fori_loop(0, STEPS, body, start, unroll=8)

    run(mixed_ref, fwd_ref, [zf_ref[m] * lift(enter_f, m) for m in range(MODES)], False)
    for p in range(4):
        turned = from_steps(fwd_ref, p)
        for b in range(2):
            cols = slice((p + 4 * b) * LANES, (p + 4 * b + 1) * LANES)
            part = turned[b * HALF : (b + 1) * HALF]
            gq_ref[:, cols] = (g_ref[:, cols].astype(F32) * part).astype(jnp.bfloat16)
    copy_q = pltpu.make_async_copy(gq_ref, gq_any, sems.at[0])
    copy_q.start()
    run(back_ref, bwd_ref, [zb_ref[m] * lift(enter_b, m) for m in range(MODES)], True)
    for p in range(4):
        turned = from_steps(bwd_ref, p)
        for b in range(2):
            cols = slice((p + 4 * b) * LANES, (p + 4 * b + 1) * LANES)
            part = turned[b * HALF : (b + 1) * HALF]
            gk_ref[:, cols] = (v_ref[:, cols].astype(F32) * part).astype(jnp.bfloat16)
            gv_ref[:, cols] = (k_ref[:, cols].astype(F32) * part).astype(jnp.bfloat16)
    copy_k = pltpu.make_async_copy(gk_ref, gk_any, sems.at[1])
    copy_v = pltpu.make_async_copy(gv_ref, gv_any, sems.at[2])
    copy_k.start()
    copy_v.start()
    copy_q.wait()
    copy_k.wait()
    copy_v.wait()


VMEM = pl.BlockSpec(memory_space=pltpu.VMEM)
SMEM = pl.BlockSpec(memory_space=pltpu.SMEM)
ANY = pl.BlockSpec(memory_space=pl.ANY)
PARAMS = pltpu.CompilerParams(vmem_limit_bytes=32 * 1024 * 1024)
MESSAGE = jax.ShapeDtypeStruct((GROUP, 2 * MODES, LANES), F32)
STATES = jax.ShapeDtypeStruct((MODES, SUB, LANES), F32)
STEPPED = jax.ShapeDtypeStruct((PITCH * SUB, LANES), F32)


def shards(queries, keys, values, grad_out, residues, decay_rate, skip_gain):
    rate = decay_rate.T
    gain = jnp.sqrt(-jnp.expm1(-2.0 * rate))
    weight = residues.T * gain
    me = lax.axis_index("ctx")
    place = jnp.stack([me % GROUP, me // GROUP]).astype(jnp.int32)
    near = [[z * GROUP + k for k in range(GROUP)] for z in range(GROUP)]
    far = [[z * GROUP + k for z in range(GROUP)] for k in range(GROUP)]
    wide = jax.ShapeDtypeStruct(queries.shape, jnp.bfloat16)
    held = pltpu.VMEM(queries.shape, jnp.bfloat16)

    stepped = pltpu.VMEM(STEPPED.shape, F32)
    states = pltpu.VMEM(STATES.shape, F32)
    ut, st, sf, xb, msg = pl.pallas_call(
        summary_kernel,
        out_shape=(STEPPED, STEPPED, STATES, STATES, MESSAGE),
        in_specs=[ANY] * 5,
        out_specs=(ANY,) * 5,
        scratch_shapes=[held] * 4
        + [pltpu.VMEM((MODES, HALF), F32), stepped, stepped, states, states]
        + [pltpu.VMEM(MESSAGE.shape[1:], F32), pltpu.VMEM((3, MODES, LANES), F32)]
        + [pltpu.VMEM((MODES, 5, SUB, LANES), F32)]
        + [pltpu.SemaphoreType.DMA((n,)) for n in (5, 4, GROUP)],
        name="summary",
    )(queries, keys, values, grad_out, rate)
    got = lax.all_to_all(msg, "ctx", 0, 0, axis_index_groups=near)
    mixed, back, zf, zb, table, near_at, far_at = pl.pallas_call(
        local_kernel,
        out_shape=(STEPPED, STEPPED, STATES, STATES)
        + tuple(jax.ShapeDtypeStruct((n, MODES, LANES), F32) for n in (5, GROUP, GROUP)),
        in_specs=[SMEM] + [VMEM] * 8,
        out_specs=(VMEM,) * 7,
        compiler_params=PARAMS,
        cost_estimate=pl.CostEstimate(
            flops=8 * STEPS * MODES * SUB * LANES, bytes_accessed=1 << 20, transcendentals=0
        ),
        name="local",
    )(place, ut, st, sf, xb, rate, weight, gain, skip_gain.reshape(1, HALF))
    msg, enter = pl.pallas_call(
        middle_kernel,
        out_shape=(MESSAGE, jax.ShapeDtypeStruct((MODES, LANES), F32)),
        in_specs=[VMEM] * 3,
        out_specs=(VMEM,) * 2,
        compiler_params=PARAMS,
        name="middle",
    )(got, table, near_at)
    got = lax.all_to_all(msg, "ctx", 0, 0, axis_index_groups=far)
    grad_q, grad_k, grad_v, grad_res, grad_skip = pl.pallas_call(
        final_kernel,
        out_shape=(
            wide,
            wide,
            wide,
            jax.ShapeDtypeStruct((MODES, HALF), F32),
            jax.ShapeDtypeStruct((1, HALF), F32),
        ),
        in_specs=[VMEM] * 11,
        out_specs=(ANY,) * 3 + (VMEM,) * 2,
        scratch_shapes=[held] * 3 + [stepped, stepped, pltpu.SemaphoreType.DMA((3,))],
        compiler_params=PARAMS,
        name="final",
    )(got, enter, table, far_at, zf, zb, mixed, back, keys, values, grad_out)
    return (grad_q, grad_k, grad_v, grad_res.T, grad_skip.reshape(HALF))


def solution(mesh):
    in_specs = (
        P("tp", "ctx"),
        P("tp", "ctx"),
        P("tp", "ctx"),
        P("tp", "ctx"),
        P("tp", None),
        P("tp", None),
        P("tp"),
    )
    out_specs = (P("tp", "ctx"), P("tp", "ctx"), P("tp", "ctx"), P("tp", None), P("tp"))
    return jax.shard_map(shards, mesh=mesh, in_specs=in_specs, out_specs=out_specs, check_vma=False)
```

```python
import math

import jax
import jax.numpy as jnp
from jax import lax
from jax.experimental import pallas as pl
from jax.experimental.pallas import tpu as pltpu
from jax.sharding import PartitionSpec as P

MODES = 16
LANES = 128
SUB = 8
HALF = 64
STEPS = 64
PITCH = STEPS + 1
CHUNKS = 16
LOCAL = STEPS * CHUNKS
GROUP = 8
TALL = 16
UNITS = 0
SIGNAL = UNITS + PITCH * SUB
FORWARD = SIGNAL + PITCH * SUB
BACKWARD = FORWARD + MODES * SUB
RATES = BACKWARD + MODES * SUB
GAINS = RATES + MODES
WEIGHTS = GAINS + MODES
SKIPS = WEIGHTS + MODES
PACK = SKIPS + SUB
SUMS = MODES
DIRECT = SUMS + MODES // 2
ROWS = DIRECT + 1
F32 = jnp.float32
NORM = 1.0 / math.sqrt(65536)


def iota(shape, dim):
    return lax.broadcasted_iota(jnp.int32, shape, dim)


def twice(rows):
    return jnp.concatenate([rows, rows], axis=1)


def lift(rows, m):
    return jnp.broadcast_to(rows[m : m + 1], (SUB, LANES))


def to_steps(x, out_ref, base):
    for p in range(4):
        low = x[:, p * LANES : (p + 1) * LANES]
        high = x[:, (p + 4) * LANES : (p + 5) * LANES]
        turned = jnp.concatenate([low, high], axis=0).T
        for q in range(2):
            first = base + (2 * p + q) * PITCH
            out_ref[first : first + STEPS, :] = turned[q * STEPS : (q + 1) * STEPS]


def from_steps(ref, out_ref):
    for p in range(4):
        first = 2 * p * PITCH
        parts = [ref[first : first + STEPS, :], ref[first + PITCH : first + PITCH + STEPS, :]]
        turned = jnp.concatenate(parts, axis=0).T
        out_ref[:, p * LANES : (p + 1) * LANES] = turned[:HALF]
        out_ref[:, (p + 4) * LANES : (p + 5) * LANES] = turned[HALF:]


def turned_rows(rows):
    return jnp.concatenate([rows, jnp.zeros((LANES - MODES, LANES), F32)], axis=0).T


def step_rows(step):
    return pl.ds(step, SUB, stride=PITCH)


def packed_modes(table):
    upper = iota((SUB, LANES), 1) >= HALF
    return jnp.where(upper, table[SUB:], table[:SUB])


def write_message(msg_ref, states, sums, direct):
    for j in range(GROUP):
        first = j * ROWS
        msg_ref[first : first + MODES] = states
        msg_ref[first + SUMS : first + DIRECT] = sums
        msg_ref[first + DIRECT : first + ROWS] = direct


def one_minus_exp(x):
    series = jnp.ones_like(x)
    for n in range(9, 1, -1):
        series = 1.0 - series * (x * (1.0 / n))
    return jnp.where(x < 0.25, x * series, 1.0 - jnp.exp(-x))


def total_of(terms):
    total = terms[0]
    for term in terms[1:]:
        total = total + term
    return total


def added(terms):
    while len(terms) > 1:
        terms = [a + b for a, b in zip(terms[::2], terms[1::2])]
    return terms[0]


def summary_kernel(
    q_any, k_any, v_any, g_any, rate_any, residue_any, skip_any,
    pack_ref, msg_ref,
    q_ref, k_ref, v_ref, g_ref, rate_ref, residue_ref, skip_ref,
    row_ref, decay_ref, sems,
):
    pairs = (
        (rate_any, rate_ref), (k_any, k_ref), (v_any, v_ref), (g_any, g_ref), (q_any, q_ref),
        (residue_any, residue_ref), (skip_any, skip_ref),
    )
    copies = [pltpu.make_async_copy(a, b, sems.at[n]) for n, (a, b) in enumerate(pairs)]
    for copy in copies:
        copy.start()

    copies[0].wait()
    copies[5].wait()
    copies[6].wait()
    rates = twice(rate_ref[...])
    gains = jnp.sqrt(one_minus_exp(2.0 * rates))
    skips = jnp.concatenate([skip_ref[...], skip_ref[...]], axis=1)
    pack_ref[RATES : RATES + MODES] = rates
    pack_ref[GAINS : GAINS + MODES] = gains
    pack_ref[WEIGHTS : WEIGHTS + MODES] = twice(residue_ref[...]) * gains
    pack_ref[SKIPS : SKIPS + SUB] = jnp.broadcast_to(skips, (SUB, LANES))
    row_ref[0] = jnp.exp(-rates)
    row_ref[1] = jnp.exp(-float(STEPS * SUB) * rates)
    for i in range(STEPS // SUB):
        row_ref[2 + i] = jnp.exp(-float(SUB * i) * rates)
    row = iota((SUB, LANES), 0)
    upper = iota((SUB, LANES), 1) >= HALF
    row_f = row.astype(F32)
    chunk = jnp.where(upper, row_f + SUB, row_f)
    for m in range(MODES):
        r = pack_ref[RATES + m : RATES + m + 1, :]
        for n, d in enumerate((1, 2, 4)):
            decay_ref[m, n] = jnp.where(row >= d, jnp.exp(-float(STEPS * d) * r), 0.0)
        decay_ref[m, 3] = jnp.where(upper, jnp.exp(-(STEPS * row_f) * r), 0.0)
        decay_ref[m, 4] = jnp.exp(-(STEPS * chunk) * r)

    copies[1].wait()
    copies[2].wait()
    to_steps(k_ref[...].astype(F32) * v_ref[...].astype(F32), pack_ref, UNITS)
    copies[3].wait()
    copies[4].wait()
    to_steps(g_ref[...].astype(F32) * q_ref[...].astype(F32), pack_ref, SIGNAL)

    zero = jnp.zeros((SUB, LANES), F32)
    ends, adjoints, totals = [], [], []
    lags = [zero] * SUB
    for half in range(2):
        modes = range(half * 8, half * 8 + 8)
        factor = [jnp.exp(-lift(pack_ref, RATES + m)) for m in modes]

        def body(i, carry):
            state, total, back, lags = carry
            u = [pack_ref[step_rows(UNITS + i * SUB + t), :] for t in range(SUB)]
            s = [pack_ref[step_rows(SIGNAL + i * SUB + t), :] for t in range(SUB)]
            part = [s[SUB - 1]] * 8
            for t in reversed(range(SUB - 1)):
                part = [f * p + s[t] for f, p in zip(factor, part)]
            total = [t + x * p for t, x, p in zip(total, state, part)]
            power = [row_ref[2 + i, m : m + 1, :] for m in modes]
            back = [b + w * p for b, w, p in zip(back, power, part)]
            for t in range(SUB):
                state = [f * x + u[t] for f, x in zip(factor, state)]
            if half == 0:
                lags = [
                    lags[d] + total_of([s[t] * u[t - d] for t in range(d, SUB)])
                    for d in range(SUB)
                ]
            return state, total, back, lags

        carry = ([zero] * 8, [zero] * 8, [zero] * 8, lags if half == 0 else [])
        state, total, back, found = lax.fori_loop(0, STEPS // SUB, body, carry, unroll=2)
        if half == 0:
            lags = found
        for n, m in enumerate(modes):
            within = lags[SUB - 1]
            for d in reversed(range(SUB - 1)):
                within = factor[n] * within + lags[d]
            scan = state[n]
            for j, d in enumerate((1, 2, 4)):
                scan = scan + decay_ref[m, j] * pltpu.roll(scan, d, 0)
            last = scan[SUB - 1 : SUB]
            last_other = pltpu.roll(last, HALF, 1)
            start = jnp.where(row >= 1, pltpu.roll(scan, 1, 0), 0.0)
            start = start + decay_ref[m, 3] * last_other
            pack_ref[FORWARD + m * SUB : FORWARD + (m + 1) * SUB] = start
            pack_ref[BACKWARD + m * SUB : BACKWARD + (m + 1) * SUB] = back[n]
            ends.append(last + row_ref[1, m : m + 1, :] * last_other)
            adjoints.append(jnp.sum(decay_ref[m, 4] * back[n], axis=0, keepdims=True))
            cross = factor[n] * (total[n] + start * back[n])
            totals.append(jnp.sum(within + cross, axis=0, keepdims=True))
    ends = jnp.concatenate(ends, axis=0)
    adjoints = jnp.concatenate(adjoints, axis=0)
    totals = jnp.concatenate(totals, axis=0)
    direct = jnp.sum(lags[0], axis=0, keepdims=True)
    adjoints = adjoints + pltpu.roll(adjoints, HALF, 1)
    totals = totals + pltpu.roll(totals, HALF, 1)
    direct = direct + pltpu.roll(direct, HALF, 1)
    lanes_up = iota((MODES, LANES), 1) >= HALF
    write_message(
        msg_ref, jnp.where(lanes_up, ends, adjoints), packed_modes(totals), direct
    )


def local_kernel(
    place_ref, pack_ref,
    mixed_ref, back_ref, after_ref, before_ref, block_ref, table_ref, near_ref, far_ref,
    steps_ref,
):
    rates = pack_ref[RATES : RATES + MODES]
    skip = pack_ref[SKIPS : SKIPS + SUB]
    wide = [lift(rates, m) for m in range(MODES)]
    factor = [jnp.exp(-r) for r in wide]
    weight = [lift(pack_ref, WEIGHTS + m) for m in range(MODES)]

    def run(source, dst_ref, start, flip):
        def body(i, state):
            step = STEPS - 1 - i if flip else i
            x = pack_ref[step_rows(source + step), :]
            state = [f * z + x for f, z in zip(factor, state)]
            dst_ref[step_rows(step), :] = (
                added([w * z for w, z in zip(weight, state)]) + skip * x
            )
            return state

        lax.fori_loop(0, STEPS, body, start, unroll=8)

    row = iota((SUB, LANES), 0)
    upper = iota((SUB, LANES), 1) >= HALF
    run(
        UNITS, steps_ref,
        [pack_ref[FORWARD + m * SUB : FORWARD + (m + 1) * SUB] for m in range(MODES)], False,
    )
    from_steps(steps_ref, mixed_ref)
    start_b = []
    for m in range(MODES):
        scan = pack_ref[BACKWARD + m * SUB : BACKWARD + (m + 1) * SUB]
        for d in (1, 2, 4):
            decay = jnp.where(row < SUB - d, jnp.exp(-float(STEPS * d) * wide[m]), 0.0)
            scan = scan + decay * pltpu.roll(scan, SUB - d, 0)
        first_other = pltpu.roll(lift(scan, 0), HALF, 1)
        start = jnp.where(row < SUB - 1, pltpu.roll(scan, SUB - 1, 0), 0.0)
        decay = jnp.exp(-(STEPS * (SUB - 1 - row).astype(F32)) * wide[m])
        start_b.append(start + jnp.where(upper, 0.0, decay * first_other))
    run(SIGNAL, steps_ref, start_b, True)
    from_steps(steps_ref, back_ref)

    rate_cols = turned_rows(rates)
    weight_cols = turned_rows(pack_ref[WEIGHTS : WEIGHTS + MODES])
    token = iota((HALF, LANES), 1).astype(F32)
    for m in range(MODES):
        r = jnp.broadcast_to(rate_cols[:HALF, m : m + 1], (HALF, LANES))
        w = jnp.broadcast_to(weight_cols[:HALF, m : m + 1], (HALF, LANES))
        after_ref[m] = w * jnp.exp(-(token + 1.0) * r)
        before_ref[m] = w * jnp.exp(-(LANES - token) * r)
        block_ref[m] = jnp.exp(-float(LANES) * r)
    lanes_up = iota((MODES, LANES), 1) >= HALF
    place = place_ref[0]
    ahead = jnp.where(lanes_up, place, GROUP - 1 - place).astype(F32)
    for k in range(GROUP):
        near_ref[k] = jnp.broadcast_to((place == k).astype(F32), (MODES, LANES))
        far_ref[k] = jnp.broadcast_to((place_ref[1] == k).astype(F32), (MODES, LANES))
    table_ref[0] = jnp.exp(-rates)
    table_ref[1] = jnp.exp(-float(LOCAL) * rates)
    table_ref[2] = jnp.exp(-float(LOCAL * GROUP) * rates)
    table_ref[3] = jnp.exp(-(LOCAL * ahead) * rates)
    table_ref[4] = pack_ref[GAINS : GAINS + MODES] * NORM


def combine(got_ref, factor, rho, chosen_ref):
    lanes_up = iota((MODES, LANES), 1) >= HALF
    zero = jnp.zeros((MODES, LANES), F32)
    pairs = [got_ref[k * ROWS : k * ROWS + MODES] for k in range(GROUP)]
    fwd, bwd = zero, zero
    enter_f, enter_b = zero, zero
    cross = zero
    sums = jnp.zeros((SUB, LANES), F32)
    direct = jnp.zeros((1, LANES), F32)
    for k in range(GROUP):
        enter_f = enter_f + chosen_ref[k] * fwd
        cross = cross + fwd * pltpu.roll(pairs[k], HALF, 1)
        fwd = rho * fwd + pairs[k]
        sums = sums + got_ref[k * ROWS + SUMS : k * ROWS + DIRECT]
        direct = direct + got_ref[k * ROWS + DIRECT : (k + 1) * ROWS]
    for k in reversed(range(GROUP)):
        enter_b = enter_b + chosen_ref[k] * bwd
        bwd = rho * bwd + pairs[k]
    entering = jnp.where(lanes_up, enter_f, enter_b)
    joint = jnp.where(lanes_up, fwd, bwd)
    cross = factor * cross
    cross = jnp.where(lanes_up, cross, pltpu.roll(cross, HALF, 1))
    return joint, sums + packed_modes(cross), direct, entering


def middle_kernel(got_ref, table_ref, near_ref, msg_ref, enter_ref):
    joint, sums, direct, entering = combine(got_ref, table_ref[0], table_ref[1], near_ref)
    enter_ref[...] = entering
    write_message(msg_ref, joint, sums, direct)


def final_kernel(
    got_ref, enter_ref, table_ref, far_ref, after_ref, before_ref, block_ref,
    mixed_ref, back_ref, k_ref, v_ref, g_ref,
    gq_any, gk_any, gv_any, gr_any, gs_any,
    gq_ref, gk_ref, gv_ref, gr_ref, gs_ref, enter_cols, full_ref, sems, out_sems,
):
    joint, sums, direct, outer = combine(got_ref, table_ref[0], table_ref[2], far_ref)
    enter_cols[...] = turned_rows(enter_ref[...] + table_ref[3] * outer)
    scaled = sums * packed_modes(table_ref[4])
    gr_ref[0:SUB] = scaled[:, :HALF]
    gr_ref[SUB:MODES] = scaled[:, HALF:]
    gs_ref[...] = direct[:, :HALF] * NORM
    copies = [
        pltpu.make_async_copy(gr_ref, gr_any, sems.at[0]),
        pltpu.make_async_copy(gs_ref, gs_any, sems.at[1]),
    ]
    for copy in copies:
        copy.start()

    def one_way(rows, unit_ref, local_ref, enter, blocks, slot, half):
        parts = [unit_ref[m, rows, :] * enter[:, m : m + 1] for m in range(MODES)]
        for n, b in enumerate(blocks):
            cols = slice(b * LANES, (b + 1) * LANES)
            full_ref[slot, half * SUB : (half + 1) * SUB, cols] = local_ref[rows, cols] + added(
                parts
            )
            if n < len(blocks) - 1:
                parts = [x * block_ref[m, rows, :] for m, x in enumerate(parts)]

    def out_copies(i):
        rows = pl.ds(pl.multiple_of(i * TALL, TALL), TALL)
        pairs = ((gq_ref, gq_any), (gk_ref, gk_any), (gv_ref, gv_any))
        return [
            pltpu.make_async_copy(a.at[rows, :], b.at[rows, :], out_sems.at[n, i])
            for n, (a, b) in enumerate(pairs)
        ]

    def body(i, carry):
        for half in range(2):
            first = pl.multiple_of(i * TALL + half * SUB, SUB)
            rows = pl.ds(first, SUB)
            enter_b = enter_cols[rows, :]
            enter_f = enter_cols[pl.ds(HALF + first, SUB), :]
            one_way(rows, after_ref, mixed_ref, enter_f, range(8), 0, half)
            one_way(rows, before_ref, back_ref, enter_b, range(7, -1, -1), 1, half)
        rows = pl.ds(pl.multiple_of(i * TALL, TALL), TALL)
        for b in range(8):
            cols = slice(b * LANES, (b + 1) * LANES)
            mixed, back = full_ref[0, :, cols], full_ref[1, :, cols]
            gq_ref[rows, cols] = (g_ref[rows, cols].astype(F32) * mixed).astype(jnp.bfloat16)
            gk_ref[rows, cols] = (v_ref[rows, cols].astype(F32) * back).astype(jnp.bfloat16)
            gv_ref[rows, cols] = (k_ref[rows, cols].astype(F32) * back).astype(jnp.bfloat16)
        for copy in out_copies(i):
            copy.start()
        return carry

    lax.fori_loop(0, HALF // TALL, body, 0, unroll=4)
    for i in range(HALF // TALL):
        copies.extend(out_copies(i))
    for copy in copies:
        copy.wait()


VMEM = pl.BlockSpec(memory_space=pltpu.VMEM)
SMEM = pl.BlockSpec(memory_space=pltpu.SMEM)
ANY = pl.BlockSpec(memory_space=pl.ANY)
PARAMS = pltpu.CompilerParams(vmem_limit_bytes=32 * 1024 * 1024)
MESSAGE = jax.ShapeDtypeStruct((GROUP * ROWS, LANES), F32)


def exchange(msg, groups):
    rows = msg.reshape(GROUP * ROWS, 1, LANES)
    rows = lax.all_to_all(rows, "ctx", 0, 0, axis_index_groups=groups, tiled=True)
    return rows.reshape(GROUP * ROWS, LANES)


def shards(queries, keys, values, grad_out, residues, decay_rate, skip_gain):
    me = lax.axis_index("ctx")
    place = jnp.stack([me % GROUP, me // GROUP]).astype(jnp.int32)
    near = [[z * GROUP + k for k in range(GROUP)] for z in range(GROUP)]
    far = [[z * GROUP + k for z in range(GROUP)] for k in range(GROUP)]
    wide = jax.ShapeDtypeStruct(queries.shape, jnp.bfloat16)
    held = pltpu.VMEM(queries.shape, jnp.bfloat16)

    stepped = pltpu.VMEM((PITCH * SUB, LANES), F32)
    small = pltpu.VMEM((MODES, HALF), F32)
    packed = jax.ShapeDtypeStruct((PACK, LANES), F32)
    sources = (
        queries, keys, values, grad_out,
        decay_rate.T, residues.T, skip_gain.reshape(1, HALF),
    )
    pack, msg = pl.pallas_call(
        summary_kernel,
        out_shape=(packed, MESSAGE),
        in_specs=[ANY] * 7,
        out_specs=(VMEM,) * 2,
        scratch_shapes=[held] * 4
        + [small, small, pltpu.VMEM((1, HALF), F32)]
        + [pltpu.VMEM((2 + STEPS // SUB, MODES, LANES), F32)]
        + [pltpu.VMEM((MODES, 5, SUB, LANES), F32), pltpu.SemaphoreType.DMA((7,))],
        compiler_params=PARAMS,
        name="summary",
    )(*(pltpu.with_memory_space_constraint(x, pltpu.HBM) for x in sources))
    got = exchange(msg, near)
    natural = jax.ShapeDtypeStruct(queries.shape, F32)
    units = jax.ShapeDtypeStruct((MODES, HALF, LANES), F32)
    mixed, back, after, before, block, table, near_at, far_at = pl.pallas_call(
        local_kernel,
        out_shape=(natural, natural, units, units, units)
        + tuple(jax.ShapeDtypeStruct((n, MODES, LANES), F32) for n in (5, GROUP, GROUP)),
        in_specs=[SMEM, VMEM],
        out_specs=(VMEM,) * 8,
        scratch_shapes=[stepped],
        compiler_params=PARAMS,
        cost_estimate=pl.CostEstimate(
            flops=8 * STEPS * MODES * SUB * LANES, bytes_accessed=1 << 20, transcendentals=0
        ),
        name="local",
    )(place, pack)
    msg, enter = pl.pallas_call(
        middle_kernel,
        out_shape=(MESSAGE, jax.ShapeDtypeStruct((MODES, LANES), F32)),
        in_specs=[VMEM] * 3,
        out_specs=(VMEM,) * 2,
        compiler_params=PARAMS,
        name="middle",
    )(got, table, near_at)
    got = exchange(msg, far)
    grad_q, grad_k, grad_v, grad_res, grad_skip = pl.pallas_call(
        final_kernel,
        out_shape=(
            wide,
            wide,
            wide,
            jax.ShapeDtypeStruct((MODES, HALF), F32),
            jax.ShapeDtypeStruct((1, HALF), F32),
        ),
        in_specs=[VMEM] * 12,
        out_specs=(ANY,) * 5,
        scratch_shapes=[held] * 3
        + [small, pltpu.VMEM((1, HALF), F32), pltpu.VMEM((LANES, LANES), F32)]
        + [pltpu.VMEM((2, TALL, queries.shape[1]), F32)]
        + [pltpu.SemaphoreType.DMA((2,)), pltpu.SemaphoreType.DMA((3, HALF // TALL))],
        compiler_params=PARAMS,
        name="final",
    )(got, enter, table, far_at, after, before, block, mixed, back, keys, values, grad_out)
    return (grad_q, grad_k, grad_v, grad_res.T, grad_skip.reshape(HALF))


def solution(mesh):
    in_specs = (
        P("tp", "ctx"),
        P("tp", "ctx"),
        P("tp", "ctx"),
        P("tp", "ctx"),
        P("tp", None),
        P("tp", None),
        P("tp"),
    )
    out_specs = (P("tp", "ctx"), P("tp", "ctx"), P("tp", "ctx"), P("tp", None), P("tp"))
    return jax.shard_map(shards, mesh=mesh, in_specs=in_specs, out_specs=out_specs, check_vma=False)
```

```python
import math

import jax
import jax.numpy as jnp
from jax import lax
from jax.experimental import pallas as pl
from jax.experimental.pallas import tpu as pltpu
from jax.sharding import PartitionSpec as P

MODES = 16
LANES = 128
SUB = 8
HALF = 64
STEPS = 64
PITCH = STEPS + 1
CHUNKS = 16
LOCAL = STEPS * CHUNKS
GROUP = 8
NEAR_ORDER = tuple((k + 5) % GROUP for k in range(GROUP))
FAR_ORDER = tuple((k + 5) % GROUP for k in range(GROUP))
TALL = 16
UNITS = 0
SIGNAL = UNITS + PITCH * SUB
FORWARD = SIGNAL + PITCH * SUB
BACKWARD = FORWARD + MODES * SUB
RATES = BACKWARD + MODES * SUB
GAINS = RATES + MODES
WEIGHTS = GAINS + MODES
SKIPS = WEIGHTS + MODES
PACK = SKIPS + SUB
SUMS = MODES
DIRECT = SUMS + MODES // 2
ROWS = DIRECT + 1
F32 = jnp.float32
NORM = 1.0 / math.sqrt(65536)


def iota(shape, dim):
    return lax.broadcasted_iota(jnp.int32, shape, dim)


def twice(rows):
    return jnp.concatenate([rows, rows], axis=1)


def lift(rows, m):
    return jnp.broadcast_to(rows[m : m + 1], (SUB, LANES))


def to_steps(x, out_ref, base):
    for p in range(4):
        low = x[:, p * LANES : (p + 1) * LANES]
        high = x[:, (p + 4) * LANES : (p + 5) * LANES]
        turned = jnp.concatenate([low, high], axis=0).T
        for q in range(2):
            first = base + (2 * p + q) * PITCH
            out_ref[first : first + STEPS, :] = turned[q * STEPS : (q + 1) * STEPS]


def from_steps(ref, out_ref):
    for p in range(4):
        first = 2 * p * PITCH
        parts = [ref[first : first + STEPS, :], ref[first + PITCH : first + PITCH + STEPS, :]]
        turned = jnp.concatenate(parts, axis=0).T
        out_ref[:, p * LANES : (p + 1) * LANES] = turned[:HALF]
        out_ref[:, (p + 4) * LANES : (p + 5) * LANES] = turned[HALF:]


def turned_rows(rows):
    return jnp.concatenate([rows, jnp.zeros((LANES - MODES, LANES), F32)], axis=0).T


def step_rows(step):
    return pl.ds(step, SUB, stride=PITCH)


def packed_modes(table):
    upper = iota((SUB, LANES), 1) >= HALF
    return jnp.where(upper, table[SUB:], table[:SUB])


def write_message(msg_ref, states, sums, direct):
    for j in range(GROUP):
        first = j * ROWS
        msg_ref[first : first + MODES] = states
        msg_ref[first + SUMS : first + DIRECT] = sums
        msg_ref[first + DIRECT : first + ROWS] = direct


def one_minus_exp(x):
    series = jnp.ones_like(x)
    for n in range(9, 1, -1):
        series = 1.0 - series * (x * (1.0 / n))
    return jnp.where(x < 0.25, x * series, 1.0 - jnp.exp(-x))


def total_of(terms):
    total = terms[0]
    for term in terms[1:]:
        total = total + term
    return total


def added(terms):
    while len(terms) > 1:
        terms = [a + b for a, b in zip(terms[::2], terms[1::2])]
    return terms[0]


def summary_kernel(
    q_any, k_any, v_any, g_any, rate_any, residue_any, skip_any,
    pack_ref, msg_ref, near_ref,
    q_ref, k_ref, v_ref, g_ref, rate_ref, residue_ref, skip_ref,
    row_ref, decay_ref, sems,
):
    pairs = (
        (rate_any, rate_ref), (k_any, k_ref), (v_any, v_ref), (g_any, g_ref), (q_any, q_ref),
        (residue_any, residue_ref), (skip_any, skip_ref),
    )
    copies = [pltpu.make_async_copy(a, b, sems.at[n]) for n, (a, b) in enumerate(pairs)]
    for copy in copies:
        copy.start()

    copies[0].wait()
    copies[5].wait()
    copies[6].wait()
    rates = twice(rate_ref[...])
    gains = jnp.sqrt(one_minus_exp(2.0 * rates))
    skips = jnp.concatenate([skip_ref[...], skip_ref[...]], axis=1)
    pack_ref[RATES : RATES + MODES] = rates
    pack_ref[GAINS : GAINS + MODES] = gains
    pack_ref[WEIGHTS : WEIGHTS + MODES] = twice(residue_ref[...]) * gains
    pack_ref[SKIPS : SKIPS + SUB] = jnp.broadcast_to(skips, (SUB, LANES))
    row_ref[0] = jnp.exp(-rates)
    near_ref[0] = jnp.exp(-rates)
    near_ref[1] = jnp.exp(-float(LOCAL) * rates)
    row_ref[1] = jnp.exp(-float(STEPS * SUB) * rates)
    for i in range(STEPS // SUB):
        row_ref[2 + i] = jnp.exp(-float(SUB * i) * rates)
    row = iota((SUB, LANES), 0)
    upper = iota((SUB, LANES), 1) >= HALF
    row_f = row.astype(F32)
    chunk = jnp.where(upper, row_f + SUB, row_f)
    for m in range(MODES):
        r = pack_ref[RATES + m : RATES + m + 1, :]
        for n, d in enumerate((1, 2, 4)):
            decay_ref[m, n] = jnp.where(row >= d, jnp.exp(-float(STEPS * d) * r), 0.0)
        decay_ref[m, 3] = jnp.where(upper, jnp.exp(-(STEPS * row_f) * r), 0.0)
        decay_ref[m, 4] = jnp.exp(-(STEPS * chunk) * r)

    copies[1].wait()
    copies[2].wait()
    to_steps(k_ref[...].astype(F32) * v_ref[...].astype(F32), pack_ref, UNITS)
    copies[3].wait()
    copies[4].wait()
    to_steps(g_ref[...].astype(F32) * q_ref[...].astype(F32), pack_ref, SIGNAL)

    zero = jnp.zeros((SUB, LANES), F32)
    ends, adjoints, totals = [], [], []
    lags = [zero] * SUB
    for half in range(2):
        modes = range(half * 8, half * 8 + 8)
        factor = [jnp.exp(-lift(pack_ref, RATES + m)) for m in modes]

        def body(i, carry):
            state, total, back, lags = carry
            u = [pack_ref[step_rows(UNITS + i * SUB + t), :] for t in range(SUB)]
            s = [pack_ref[step_rows(SIGNAL + i * SUB + t), :] for t in range(SUB)]
            part = [s[SUB - 1]] * 8
            for t in reversed(range(SUB - 1)):
                part = [f * p + s[t] for f, p in zip(factor, part)]
            total = [t + x * p for t, x, p in zip(total, state, part)]
            power = [row_ref[2 + i, m : m + 1, :] for m in modes]
            back = [b + w * p for b, w, p in zip(back, power, part)]
            for t in range(SUB):
                state = [f * x + u[t] for f, x in zip(factor, state)]
            if half == 0:
                lags = [
                    lags[d] + total_of([s[t] * u[t - d] for t in range(d, SUB)])
                    for d in range(SUB)
                ]
            return state, total, back, lags

        carry = ([zero] * 8, [zero] * 8, [zero] * 8, lags if half == 0 else [])
        state, total, back, found = lax.fori_loop(0, STEPS // SUB, body, carry, unroll=2)
        if half == 0:
            lags = found
        for n, m in enumerate(modes):
            within = lags[SUB - 1]
            for d in reversed(range(SUB - 1)):
                within = factor[n] * within + lags[d]
            scan = state[n]
            for j, d in enumerate((1, 2, 4)):
                scan = scan + decay_ref[m, j] * pltpu.roll(scan, d, 0)
            last = scan[SUB - 1 : SUB]
            last_other = pltpu.roll(last, HALF, 1)
            start = jnp.where(row >= 1, pltpu.roll(scan, 1, 0), 0.0)
            start = start + decay_ref[m, 3] * last_other
            pack_ref[FORWARD + m * SUB : FORWARD + (m + 1) * SUB] = start
            pack_ref[BACKWARD + m * SUB : BACKWARD + (m + 1) * SUB] = back[n]
            ends.append(last + row_ref[1, m : m + 1, :] * last_other)
            adjoints.append(jnp.sum(decay_ref[m, 4] * back[n], axis=0, keepdims=True))
            cross = factor[n] * (total[n] + start * back[n])
            totals.append(jnp.sum(within + cross, axis=0, keepdims=True))
    ends = jnp.concatenate(ends, axis=0)
    adjoints = jnp.concatenate(adjoints, axis=0)
    totals = jnp.concatenate(totals, axis=0)
    direct = jnp.sum(lags[0], axis=0, keepdims=True)
    adjoints = adjoints + pltpu.roll(adjoints, HALF, 1)
    totals = totals + pltpu.roll(totals, HALF, 1)
    direct = direct + pltpu.roll(direct, HALF, 1)
    lanes_up = iota((MODES, LANES), 1) >= HALF
    write_message(
        msg_ref, jnp.where(lanes_up, ends, adjoints), packed_modes(totals), direct
    )


def local_kernel(
    pack_ref,
    mixed_ref, back_ref, after_ref, before_ref, block_ref, table_ref,
    steps_ref,
):
    rates = pack_ref[RATES : RATES + MODES]
    skip = pack_ref[SKIPS : SKIPS + SUB]
    wide = [lift(rates, m) for m in range(MODES)]
    factor = [jnp.exp(-r) for r in wide]
    weight = [lift(pack_ref, WEIGHTS + m) for m in range(MODES)]

    def run(source, dst_ref, start, flip):
        def body(i, state):
            step = STEPS - 1 - i if flip else i
            x = pack_ref[step_rows(source + step), :]
            state = [f * z + x for f, z in zip(factor, state)]
            dst_ref[step_rows(step), :] = (
                added([w * z for w, z in zip(weight, state)]) + skip * x
            )
            return state

        lax.fori_loop(0, STEPS, body, start, unroll=8)

    row = iota((SUB, LANES), 0)
    upper = iota((SUB, LANES), 1) >= HALF
    run(
        UNITS, steps_ref,
        [pack_ref[FORWARD + m * SUB : FORWARD + (m + 1) * SUB] for m in range(MODES)], False,
    )
    from_steps(steps_ref, mixed_ref)
    start_b = []
    for m in range(MODES):
        scan = pack_ref[BACKWARD + m * SUB : BACKWARD + (m + 1) * SUB]
        for d in (1, 2, 4):
            decay = jnp.where(row < SUB - d, jnp.exp(-float(STEPS * d) * wide[m]), 0.0)
            scan = scan + decay * pltpu.roll(scan, SUB - d, 0)
        first_other = pltpu.roll(lift(scan, 0), HALF, 1)
        start = jnp.where(row < SUB - 1, pltpu.roll(scan, SUB - 1, 0), 0.0)
        decay = jnp.exp(-(STEPS * (SUB - 1 - row).astype(F32)) * wide[m])
        start_b.append(start + jnp.where(upper, 0.0, decay * first_other))
    run(SIGNAL, steps_ref, start_b, True)
    from_steps(steps_ref, back_ref)

    rate_cols = turned_rows(rates)
    weight_cols = turned_rows(pack_ref[WEIGHTS : WEIGHTS + MODES])
    token = iota((HALF, LANES), 1).astype(F32)
    for m in range(MODES):
        r = jnp.broadcast_to(rate_cols[:HALF, m : m + 1], (HALF, LANES))
        w = jnp.broadcast_to(weight_cols[:HALF, m : m + 1], (HALF, LANES))
        after_ref[m] = w * jnp.exp(-(token + 1.0) * r)
        before_ref[m] = w * jnp.exp(-(LANES - token) * r)
        block_ref[m] = jnp.exp(-float(LANES) * r)
    lanes_up = iota((MODES, LANES), 1) >= HALF
    place = lax.rem(lax.axis_index("ctx"), GROUP)
    ahead = jnp.where(lanes_up, place, GROUP - 1 - place).astype(F32)
    table_ref[0] = jnp.exp(-rates)
    table_ref[1] = jnp.exp(-float(LOCAL * GROUP) * rates)
    table_ref[2] = jnp.exp(-(LOCAL * ahead) * rates)
    table_ref[3] = pack_ref[GAINS : GAINS + MODES] * NORM


def combine(got_ref, order, factor, rho, place):
    lanes_up = iota((MODES, LANES), 1) >= HALF
    zero = jnp.zeros((MODES, LANES), F32)
    firsts = [order.index(k) * ROWS for k in range(GROUP)]
    pairs = [got_ref[f : f + MODES] for f in firsts]
    fwd, bwd = zero, zero
    enter_f, enter_b = zero, zero
    cross = zero
    sums = jnp.zeros((SUB, LANES), F32)
    direct = jnp.zeros((1, LANES), F32)
    for k in range(GROUP):
        enter_f = jnp.where(place == k, fwd, enter_f)
        cross = cross + fwd * pltpu.roll(pairs[k], HALF, 1)
        fwd = rho * fwd + pairs[k]
        sums = sums + got_ref[firsts[k] + SUMS : firsts[k] + DIRECT]
        direct = direct + got_ref[firsts[k] + DIRECT : firsts[k] + ROWS]
    for k in reversed(range(GROUP)):
        enter_b = jnp.where(place == k, bwd, enter_b)
        bwd = rho * bwd + pairs[k]
    entering = jnp.where(lanes_up, enter_f, enter_b)
    joint = jnp.where(lanes_up, fwd, bwd)
    cross = factor * cross
    cross = jnp.where(lanes_up, cross, pltpu.roll(cross, HALF, 1))
    return joint, sums + packed_modes(cross), direct, entering


def middle_kernel(got_ref, near_ref, msg_ref, enter_ref):
    joint, sums, direct, entering = combine(
        got_ref, NEAR_ORDER, near_ref[0], near_ref[1], lax.rem(lax.axis_index("ctx"), GROUP)
    )
    enter_ref[...] = entering
    write_message(msg_ref, joint, sums, direct)


def final_kernel(
    got_ref, enter_ref, table_ref, after_ref, before_ref, block_ref,
    mixed_ref, back_ref, k_ref, v_ref, g_ref,
    gq_any, gk_any, gv_any, gr_any, gs_any,
    gq_ref, gk_ref, gv_ref, gr_ref, gs_ref, enter_cols, full_ref, sems, out_sems,
):
    joint, sums, direct, outer = combine(
        got_ref, FAR_ORDER, table_ref[0], table_ref[1], lax.div(lax.axis_index("ctx"), GROUP)
    )
    enter_cols[...] = turned_rows(enter_ref[...] + table_ref[2] * outer)
    scaled = sums * packed_modes(table_ref[3])
    gr_ref[0:SUB] = scaled[:, :HALF]
    gr_ref[SUB:MODES] = scaled[:, HALF:]
    gs_ref[...] = direct[:, :HALF] * NORM
    copies = [
        pltpu.make_async_copy(gr_ref, gr_any, sems.at[0]),
        pltpu.make_async_copy(gs_ref, gs_any, sems.at[1]),
    ]
    for copy in copies:
        copy.start()

    def one_way(rows, unit_ref, local_ref, enter, blocks, slot, half):
        parts = [unit_ref[m, rows, :] * enter[:, m : m + 1] for m in range(MODES)]
        for n, b in enumerate(blocks):
            cols = slice(b * LANES, (b + 1) * LANES)
            full_ref[slot, half * SUB : (half + 1) * SUB, cols] = local_ref[rows, cols] + added(
                parts
            )
            if n < len(blocks) - 1:
                parts = [x * block_ref[m, rows, :] for m, x in enumerate(parts)]

    def out_copies(i):
        rows = pl.ds(pl.multiple_of(i * TALL, TALL), TALL)
        pairs = ((gq_ref, gq_any), (gk_ref, gk_any), (gv_ref, gv_any))
        return [
            pltpu.make_async_copy(a.at[rows, :], b.at[rows, :], out_sems.at[n, i])
            for n, (a, b) in enumerate(pairs)
        ]

    def body(i, carry):
        for half in range(2):
            first = pl.multiple_of(i * TALL + half * SUB, SUB)
            rows = pl.ds(first, SUB)
            enter_b = enter_cols[rows, :]
            enter_f = enter_cols[pl.ds(HALF + first, SUB), :]
            one_way(rows, after_ref, mixed_ref, enter_f, range(8), 0, half)
            one_way(rows, before_ref, back_ref, enter_b, range(7, -1, -1), 1, half)
        rows = pl.ds(pl.multiple_of(i * TALL, TALL), TALL)
        for b in range(8):
            cols = slice(b * LANES, (b + 1) * LANES)
            mixed, back = full_ref[0, :, cols], full_ref[1, :, cols]
            gq_ref[rows, cols] = (g_ref[rows, cols].astype(F32) * mixed).astype(jnp.bfloat16)
            gk_ref[rows, cols] = (v_ref[rows, cols].astype(F32) * back).astype(jnp.bfloat16)
            gv_ref[rows, cols] = (k_ref[rows, cols].astype(F32) * back).astype(jnp.bfloat16)
        for copy in out_copies(i):
            copy.start()
        return carry

    lax.fori_loop(0, HALF // TALL, body, 0, unroll=4)
    for i in range(HALF // TALL):
        copies.extend(out_copies(i))
    for copy in copies:
        copy.wait()


VMEM = pl.BlockSpec(memory_space=pltpu.VMEM)
ANY = pl.BlockSpec(memory_space=pl.ANY)
PARAMS = pltpu.CompilerParams(vmem_limit_bytes=32 * 1024 * 1024)
MESSAGE = jax.ShapeDtypeStruct((GROUP * ROWS, LANES), F32)


def exchange(msg, groups):
    rows = msg.reshape(GROUP * ROWS, 1, LANES)
    rows = lax.all_to_all(rows, "ctx", 0, 0, axis_index_groups=groups, tiled=True)
    return rows.reshape(GROUP * ROWS, LANES)


def shards(queries, keys, values, grad_out, residues, decay_rate, skip_gain):
    near = [[z * GROUP + k for k in NEAR_ORDER] for z in range(GROUP)]
    far = [[z * GROUP + k for z in FAR_ORDER] for k in range(GROUP)]
    wide = jax.ShapeDtypeStruct(queries.shape, jnp.bfloat16)
    held = pltpu.VMEM(queries.shape, jnp.bfloat16)

    stepped = pltpu.VMEM((PITCH * SUB, LANES), F32)
    small = pltpu.VMEM((MODES, HALF), F32)
    packed = jax.ShapeDtypeStruct((PACK, LANES), F32)
    sources = (
        queries, keys, values, grad_out,
        decay_rate.T, residues.T, skip_gain.reshape(1, HALF),
    )
    pack, msg, near_table = pl.pallas_call(
        summary_kernel,
        out_shape=(packed, MESSAGE, jax.ShapeDtypeStruct((2, MODES, LANES), F32)),
        in_specs=[ANY] * 7,
        out_specs=(VMEM,) * 3,
        scratch_shapes=[held] * 4
        + [small, small, pltpu.VMEM((1, HALF), F32)]
        + [pltpu.VMEM((2 + STEPS // SUB, MODES, LANES), F32)]
        + [pltpu.VMEM((MODES, 5, SUB, LANES), F32), pltpu.SemaphoreType.DMA((7,))],
        compiler_params=PARAMS,
        name="summary",
    )(*(pltpu.with_memory_space_constraint(x, pltpu.HBM) for x in sources))
    got = exchange(msg, near)
    msg, enter = pl.pallas_call(
        middle_kernel,
        out_shape=(MESSAGE, jax.ShapeDtypeStruct((MODES, LANES), F32)),
        in_specs=[VMEM] * 2,
        out_specs=(VMEM,) * 2,
        compiler_params=PARAMS,
        name="middle",
    )(got, near_table)
    pack, enter = lax.optimization_barrier((pack, enter))
    natural = jax.ShapeDtypeStruct(queries.shape, F32)
    units = jax.ShapeDtypeStruct((MODES, HALF, LANES), F32)
    mixed, back, after, before, block, table = pl.pallas_call(
        local_kernel,
        out_shape=(natural, natural, units, units, units)
        + (jax.ShapeDtypeStruct((4, MODES, LANES), F32),),
        in_specs=[VMEM],
        out_specs=(VMEM,) * 6,
        scratch_shapes=[stepped],
        compiler_params=PARAMS,
        cost_estimate=pl.CostEstimate(
            flops=8 * STEPS * MODES * SUB * LANES, bytes_accessed=1 << 20, transcendentals=0
        ),
        name="local",
    )(pack)
    got = exchange(msg, far)
    grad_q, grad_k, grad_v, grad_res, grad_skip = pl.pallas_call(
        final_kernel,
        out_shape=(
            wide,
            wide,
            wide,
            jax.ShapeDtypeStruct((MODES, HALF), F32),
            jax.ShapeDtypeStruct((1, HALF), F32),
        ),
        in_specs=[VMEM] * 11,
        out_specs=(ANY,) * 5,
        scratch_shapes=[held] * 3
        + [small, pltpu.VMEM((1, HALF), F32), pltpu.VMEM((LANES, LANES), F32)]
        + [pltpu.VMEM((2, TALL, queries.shape[1]), F32)]
        + [pltpu.SemaphoreType.DMA((2,)), pltpu.SemaphoreType.DMA((3, HALF // TALL))],
        compiler_params=PARAMS,
        name="final",
    )(got, enter, table, after, before, block, mixed, back, keys, values, grad_out)
    return (grad_q, grad_k, grad_v, grad_res.T, grad_skip.reshape(HALF))


def solution(mesh):
    in_specs = (
        P("tp", "ctx"),
        P("tp", "ctx"),
        P("tp", "ctx"),
        P("tp", "ctx"),
        P("tp", None),
        P("tp", None),
        P("tp"),
    )
    out_specs = (P("tp", "ctx"), P("tp", "ctx"), P("tp", "ctx"), P("tp", None), P("tp"))
    return jax.shard_map(shards, mesh=mesh, in_specs=in_specs, out_specs=out_specs, check_vma=False)
```

```python
import math

import jax
import jax.numpy as jnp
from jax import lax
from jax.experimental import pallas as pl
from jax.experimental.pallas import tpu as pltpu
from jax.sharding import PartitionSpec as P

MODES = 16
LANES = 128
SUB = 8
HALF = 64
STEPS = 64
PITCH = STEPS + 1
CHUNKS = 16
LOCAL = STEPS * CHUNKS
GROUP = 8
EARLY = 4
NEAR_ORDER = tuple((k + 5) % GROUP for k in range(GROUP))
FAR_ORDER = tuple((k + 5) % GROUP for k in range(GROUP))
TALL = 16
UNITS = 0
SIGNAL = UNITS + PITCH * SUB
FORWARD = SIGNAL + PITCH * SUB
BACKWARD = FORWARD + MODES * SUB
RATES = BACKWARD + MODES * SUB
GAINS = RATES + MODES
WEIGHTS = GAINS + MODES
SKIPS = WEIGHTS + MODES
PACK = SKIPS + SUB
SUMS = MODES
DIRECT = SUMS + MODES // 2
ROWS = DIRECT + 1
F32 = jnp.float32
NORM = 1.0 / math.sqrt(65536)


def iota(shape, dim):
    return lax.broadcasted_iota(jnp.int32, shape, dim)


def twice(rows):
    return jnp.concatenate([rows, rows], axis=1)


def lift(rows, m):
    return jnp.broadcast_to(rows[m : m + 1], (SUB, LANES))


def to_steps(x, out_ref, base):
    for p in range(4):
        low = x[:, p * LANES : (p + 1) * LANES]
        high = x[:, (p + 4) * LANES : (p + 5) * LANES]
        turned = jnp.concatenate([low, high], axis=0).T
        for q in range(2):
            first = base + (2 * p + q) * PITCH
            out_ref[first : first + STEPS, :] = turned[q * STEPS : (q + 1) * STEPS]


def from_steps(ref, out_ref):
    for p in range(4):
        first = 2 * p * PITCH
        parts = [ref[first : first + STEPS, :], ref[first + PITCH : first + PITCH + STEPS, :]]
        turned = jnp.concatenate(parts, axis=0).T
        out_ref[:, p * LANES : (p + 1) * LANES] = turned[:HALF]
        out_ref[:, (p + 4) * LANES : (p + 5) * LANES] = turned[HALF:]


def turned_rows(rows):
    return jnp.concatenate([rows, jnp.zeros((LANES - MODES, LANES), F32)], axis=0).T


def step_rows(step):
    return pl.ds(step, SUB, stride=PITCH)


def packed_modes(table):
    upper = iota((SUB, LANES), 1) >= HALF
    return jnp.where(upper, table[SUB:], table[:SUB])


def write_message(msg_ref, states, sums, direct):
    for j in range(GROUP):
        first = j * ROWS
        msg_ref[first : first + MODES] = states
        msg_ref[first + SUMS : first + DIRECT] = sums
        msg_ref[first + DIRECT : first + ROWS] = direct


def one_minus_exp(x):
    series = jnp.ones_like(x)
    for n in range(9, 1, -1):
        series = 1.0 - series * (x * (1.0 / n))
    return jnp.where(x < 0.25, x * series, 1.0 - jnp.exp(-x))


def total_of(terms):
    total = terms[0]
    for term in terms[1:]:
        total = total + term
    return total


def added(terms):
    while len(terms) > 1:
        terms = [a + b for a, b in zip(terms[::2], terms[1::2])]
    return terms[0]


def summary_kernel(
    q_any, k_any, v_any, g_any, rate_any, residue_any, skip_any,
    pack_ref, msg_ref, near_ref,
    q_ref, k_ref, v_ref, g_ref, rate_ref, residue_ref, skip_ref,
    row_ref, decay_ref, sems,
):
    pairs = (
        (rate_any, rate_ref), (k_any, k_ref), (v_any, v_ref), (g_any, g_ref), (q_any, q_ref),
        (residue_any, residue_ref), (skip_any, skip_ref),
    )
    copies = [pltpu.make_async_copy(a, b, sems.at[n]) for n, (a, b) in enumerate(pairs)]
    for copy in copies:
        copy.start()

    copies[0].wait()
    copies[5].wait()
    copies[6].wait()
    rates = twice(rate_ref[...])
    gains = jnp.sqrt(one_minus_exp(2.0 * rates))
    skips = jnp.concatenate([skip_ref[...], skip_ref[...]], axis=1)
    pack_ref[RATES : RATES + MODES] = rates
    pack_ref[GAINS : GAINS + MODES] = gains
    pack_ref[WEIGHTS : WEIGHTS + MODES] = twice(residue_ref[...]) * gains
    pack_ref[SKIPS : SKIPS + SUB] = jnp.broadcast_to(skips, (SUB, LANES))
    row_ref[0] = jnp.exp(-rates)
    near_ref[0] = jnp.exp(-rates)
    near_ref[1] = jnp.exp(-float(LOCAL) * rates)
    row_ref[1] = jnp.exp(-float(STEPS * SUB) * rates)
    for i in range(STEPS // SUB):
        row_ref[2 + i] = jnp.exp(-float(SUB * i) * rates)
    row = iota((SUB, LANES), 0)
    upper = iota((SUB, LANES), 1) >= HALF
    row_f = row.astype(F32)
    chunk = jnp.where(upper, row_f + SUB, row_f)
    for m in range(MODES):
        r = pack_ref[RATES + m : RATES + m + 1, :]
        for n, d in enumerate((1, 2, 4)):
            decay_ref[m, n] = jnp.where(row >= d, jnp.exp(-float(STEPS * d) * r), 0.0)
        decay_ref[m, 3] = jnp.where(upper, jnp.exp(-(STEPS * row_f) * r), 0.0)
        decay_ref[m, 4] = jnp.exp(-(STEPS * chunk) * r)

    copies[1].wait()
    copies[2].wait()
    to_steps(k_ref[...].astype(F32) * v_ref[...].astype(F32), pack_ref, UNITS)
    copies[3].wait()
    copies[4].wait()
    to_steps(g_ref[...].astype(F32) * q_ref[...].astype(F32), pack_ref, SIGNAL)

    zero = jnp.zeros((SUB, LANES), F32)
    ends, adjoints, totals = [], [], []
    lags = [zero] * SUB
    for half in range(2):
        modes = range(half * 8, half * 8 + 8)
        factor = [jnp.exp(-lift(pack_ref, RATES + m)) for m in modes]

        def body(i, carry):
            state, total, back, lags = carry
            u = [pack_ref[step_rows(UNITS + i * SUB + t), :] for t in range(SUB)]
            s = [pack_ref[step_rows(SIGNAL + i * SUB + t), :] for t in range(SUB)]
            part = [s[SUB - 1]] * 8
            for t in reversed(range(SUB - 1)):
                part = [f * p + s[t] for f, p in zip(factor, part)]
            total = [t + x * p for t, x, p in zip(total, state, part)]
            power = [row_ref[2 + i, m : m + 1, :] for m in modes]
            back = [b + w * p for b, w, p in zip(back, power, part)]
            for t in range(SUB):
                state = [f * x + u[t] for f, x in zip(factor, state)]
            if half == 0:
                lags = [
                    lags[d] + total_of([s[t] * u[t - d] for t in range(d, SUB)])
                    for d in range(SUB)
                ]
            return state, total, back, lags

        carry = ([zero] * 8, [zero] * 8, [zero] * 8, lags if half == 0 else [])
        state, total, back, found = lax.fori_loop(0, STEPS // SUB, body, carry, unroll=2)
        if half == 0:
            lags = found
        for n, m in enumerate(modes):
            within = lags[SUB - 1]
            for d in reversed(range(SUB - 1)):
                within = factor[n] * within + lags[d]
            scan = state[n]
            for j, d in enumerate((1, 2, 4)):
                scan = scan + decay_ref[m, j] * pltpu.roll(scan, d, 0)
            last = scan[SUB - 1 : SUB]
            last_other = pltpu.roll(last, HALF, 1)
            start = jnp.where(row >= 1, pltpu.roll(scan, 1, 0), 0.0)
            start = start + decay_ref[m, 3] * last_other
            pack_ref[FORWARD + m * SUB : FORWARD + (m + 1) * SUB] = start
            pack_ref[BACKWARD + m * SUB : BACKWARD + (m + 1) * SUB] = back[n]
            ends.append(last + row_ref[1, m : m + 1, :] * last_other)
            adjoints.append(jnp.sum(decay_ref[m, 4] * back[n], axis=0, keepdims=True))
            cross = factor[n] * (total[n] + start * back[n])
            totals.append(jnp.sum(within + cross, axis=0, keepdims=True))
    ends = jnp.concatenate(ends, axis=0)
    adjoints = jnp.concatenate(adjoints, axis=0)
    totals = jnp.concatenate(totals, axis=0)
    direct = jnp.sum(lags[0], axis=0, keepdims=True)
    adjoints = adjoints + pltpu.roll(adjoints, HALF, 1)
    totals = totals + pltpu.roll(totals, HALF, 1)
    direct = direct + pltpu.roll(direct, HALF, 1)
    lanes_up = iota((MODES, LANES), 1) >= HALF
    write_message(
        msg_ref, jnp.where(lanes_up, ends, adjoints), packed_modes(totals), direct
    )


def local_outputs(
    pack_ref,
    mixed_ref, back_ref, after_ref, before_ref, block_ref, table_ref,
    steps_ref,
):
    rates = pack_ref[RATES : RATES + MODES]
    skip = pack_ref[SKIPS : SKIPS + SUB]
    wide = [lift(rates, m) for m in range(MODES)]
    factor = [jnp.exp(-r) for r in wide]
    weight = [lift(pack_ref, WEIGHTS + m) for m in range(MODES)]

    def run(source, dst_ref, start, flip):
        def body(i, state):
            step = STEPS - 1 - i if flip else i
            x = pack_ref[step_rows(source + step), :]
            state = [f * z + x for f, z in zip(factor, state)]
            dst_ref[step_rows(step), :] = (
                added([w * z for w, z in zip(weight, state)]) + skip * x
            )
            return state

        lax.fori_loop(0, STEPS, body, start, unroll=8)

    row = iota((SUB, LANES), 0)
    upper = iota((SUB, LANES), 1) >= HALF
    run(
        UNITS, steps_ref,
        [pack_ref[FORWARD + m * SUB : FORWARD + (m + 1) * SUB] for m in range(MODES)], False,
    )
    from_steps(steps_ref, mixed_ref)
    start_b = []
    for m in range(MODES):
        scan = pack_ref[BACKWARD + m * SUB : BACKWARD + (m + 1) * SUB]
        for d in (1, 2, 4):
            decay = jnp.where(row < SUB - d, jnp.exp(-float(STEPS * d) * wide[m]), 0.0)
            scan = scan + decay * pltpu.roll(scan, SUB - d, 0)
        first_other = pltpu.roll(lift(scan, 0), HALF, 1)
        start = jnp.where(row < SUB - 1, pltpu.roll(scan, SUB - 1, 0), 0.0)
        decay = jnp.exp(-(STEPS * (SUB - 1 - row).astype(F32)) * wide[m])
        start_b.append(start + jnp.where(upper, 0.0, decay * first_other))
    run(SIGNAL, steps_ref, start_b, True)
    from_steps(steps_ref, back_ref)

    rate_cols = turned_rows(rates)
    weight_cols = turned_rows(pack_ref[WEIGHTS : WEIGHTS + MODES])
    token = iota((HALF, LANES), 1).astype(F32)
    for m in range(MODES):
        r = jnp.broadcast_to(rate_cols[:HALF, m : m + 1], (HALF, LANES))
        w = jnp.broadcast_to(weight_cols[:HALF, m : m + 1], (HALF, LANES))
        after_ref[m] = w * jnp.exp(-(token + 1.0) * r)
        before_ref[m] = w * jnp.exp(-(LANES - token) * r)
        block_ref[m] = jnp.exp(-float(LANES) * r)
    lanes_up = iota((MODES, LANES), 1) >= HALF
    place = lax.rem(lax.axis_index("ctx"), GROUP)
    ahead = jnp.where(lanes_up, place, GROUP - 1 - place).astype(F32)
    table_ref[0] = jnp.exp(-rates)
    table_ref[1] = jnp.exp(-float(LOCAL * GROUP) * rates)
    table_ref[2] = jnp.exp(-(LOCAL * ahead) * rates)
    table_ref[3] = pack_ref[GAINS : GAINS + MODES] * NORM


def combine(got_ref, order, factor, rho, place):
    lanes_up = iota((MODES, LANES), 1) >= HALF
    zero = jnp.zeros((MODES, LANES), F32)
    firsts = [order.index(k) * ROWS for k in range(GROUP)]
    pairs = [got_ref[f : f + MODES] for f in firsts]
    fwd, bwd = zero, zero
    enter_f, enter_b = zero, zero
    cross = zero
    sums = jnp.zeros((SUB, LANES), F32)
    direct = jnp.zeros((1, LANES), F32)
    for k in range(GROUP):
        enter_f = jnp.where(place == k, fwd, enter_f)
        cross = cross + fwd * pltpu.roll(pairs[k], HALF, 1)
        fwd = rho * fwd + pairs[k]
        sums = sums + got_ref[firsts[k] + SUMS : firsts[k] + DIRECT]
        direct = direct + got_ref[firsts[k] + DIRECT : firsts[k] + ROWS]
    for k in reversed(range(GROUP)):
        enter_b = jnp.where(place == k, bwd, enter_b)
        bwd = rho * bwd + pairs[k]
    entering = jnp.where(lanes_up, enter_f, enter_b)
    joint = jnp.where(lanes_up, fwd, bwd)
    cross = factor * cross
    cross = jnp.where(lanes_up, cross, pltpu.roll(cross, HALF, 1))
    return joint, sums + packed_modes(cross), direct, entering


def starts_early():
    return lax.div(lax.axis_index("ctx"), GROUP) < EARLY


def middle_kernel(
    got_ref, near_ref, pack_ref, msg_ref, enter_ref, *refs
):
    joint, sums, direct, entering = combine(
        got_ref, NEAR_ORDER, near_ref[0], near_ref[1], lax.rem(lax.axis_index("ctx"), GROUP)
    )
    enter_ref[...] = entering
    write_message(msg_ref, joint, sums, direct)

    @pl.when(starts_early())
    def _():
        local_outputs(pack_ref, *refs)


def final_kernel(*refs):
    got, enter, pack, *early = refs[:9]
    rest, late, steps = refs[9:-7], refs[-7:-1], refs[-1]

    @pl.when(starts_early())
    def _():
        finish(got, enter, *early, *rest)

    @pl.when(jnp.logical_not(starts_early()))
    def _():
        local_outputs(pack, *late, steps)
        finish(got, enter, *late, *rest)


def finish(
    got_ref, enter_ref, mixed_ref, back_ref, after_ref, before_ref, block_ref, table_ref,
    k_ref, v_ref, g_ref,
    gq_any, gk_any, gv_any, gr_any, gs_any,
    gq_ref, gk_ref, gv_ref, gr_ref, gs_ref, enter_cols, full_ref, sems, out_sems,
):
    joint, sums, direct, outer = combine(
        got_ref, FAR_ORDER, table_ref[0], table_ref[1], lax.div(lax.axis_index("ctx"), GROUP)
    )
    enter_cols[...] = turned_rows(enter_ref[...] + table_ref[2] * outer)
    scaled = sums * packed_modes(table_ref[3])
    gr_ref[0:SUB] = scaled[:, :HALF]
    gr_ref[SUB:MODES] = scaled[:, HALF:]
    gs_ref[...] = direct[:, :HALF] * NORM
    copies = [
        pltpu.make_async_copy(gr_ref, gr_any, sems.at[0]),
        pltpu.make_async_copy(gs_ref, gs_any, sems.at[1]),
    ]
    for copy in copies:
        copy.start()

    def one_way(rows, unit_ref, local_ref, enter, blocks, slot, half):
        parts = [unit_ref[m, rows, :] * enter[:, m : m + 1] for m in range(MODES)]
        for n, b in enumerate(blocks):
            cols = slice(b * LANES, (b + 1) * LANES)
            full_ref[slot, half * SUB : (half + 1) * SUB, cols] = local_ref[rows, cols] + added(
                parts
            )
            if n < len(blocks) - 1:
                parts = [x * block_ref[m, rows, :] for m, x in enumerate(parts)]

    def out_copies(i):
        rows = pl.ds(pl.multiple_of(i * TALL, TALL), TALL)
        pairs = ((gq_ref, gq_any), (gk_ref, gk_any), (gv_ref, gv_any))
        return [
            pltpu.make_async_copy(a.at[rows, :], b.at[rows, :], out_sems.at[n, i])
            for n, (a, b) in enumerate(pairs)
        ]

    def body(i, carry):
        for half in range(2):
            first = pl.multiple_of(i * TALL + half * SUB, SUB)
            rows = pl.ds(first, SUB)
            enter_b = enter_cols[rows, :]
            enter_f = enter_cols[pl.ds(HALF + first, SUB), :]
            one_way(rows, after_ref, mixed_ref, enter_f, range(8), 0, half)
            one_way(rows, before_ref, back_ref, enter_b, range(7, -1, -1), 1, half)
        rows = pl.ds(pl.multiple_of(i * TALL, TALL), TALL)
        for b in range(8):
            cols = slice(b * LANES, (b + 1) * LANES)
            mixed, back = full_ref[0, :, cols], full_ref[1, :, cols]
            gq_ref[rows, cols] = (g_ref[rows, cols].astype(F32) * mixed).astype(jnp.bfloat16)
            gk_ref[rows, cols] = (v_ref[rows, cols].astype(F32) * back).astype(jnp.bfloat16)
            gv_ref[rows, cols] = (k_ref[rows, cols].astype(F32) * back).astype(jnp.bfloat16)
        for copy in out_copies(i):
            copy.start()
        return carry

    lax.fori_loop(0, HALF // TALL, body, 0, unroll=4)
    for i in range(HALF // TALL):
        copies.extend(out_copies(i))
    for copy in copies:
        copy.wait()


VMEM = pl.BlockSpec(memory_space=pltpu.VMEM)
ANY = pl.BlockSpec(memory_space=pl.ANY)
PARAMS = pltpu.CompilerParams(vmem_limit_bytes=32 * 1024 * 1024)
MESSAGE = jax.ShapeDtypeStruct((GROUP * ROWS, LANES), F32)


def exchange(msg, groups):
    rows = msg.reshape(GROUP * ROWS, 1, LANES)
    rows = lax.all_to_all(rows, "ctx", 0, 0, axis_index_groups=groups, tiled=True)
    return rows.reshape(GROUP * ROWS, LANES)


def shards(queries, keys, values, grad_out, residues, decay_rate, skip_gain):
    near = [[z * GROUP + k for k in NEAR_ORDER] for z in range(GROUP)]
    far = [[z * GROUP + k for z in FAR_ORDER] for k in range(GROUP)]
    wide = jax.ShapeDtypeStruct(queries.shape, jnp.bfloat16)
    held = pltpu.VMEM(queries.shape, jnp.bfloat16)

    stepped = pltpu.VMEM((PITCH * SUB, LANES), F32)
    small = pltpu.VMEM((MODES, HALF), F32)
    packed = jax.ShapeDtypeStruct((PACK, LANES), F32)
    sources = (
        queries, keys, values, grad_out,
        decay_rate.T, residues.T, skip_gain.reshape(1, HALF),
    )
    pack, msg, near_table = pl.pallas_call(
        summary_kernel,
        out_shape=(packed, MESSAGE, jax.ShapeDtypeStruct((2, MODES, LANES), F32)),
        in_specs=[ANY] * 7,
        out_specs=(VMEM,) * 3,
        scratch_shapes=[held] * 4
        + [small, small, pltpu.VMEM((1, HALF), F32)]
        + [pltpu.VMEM((2 + STEPS // SUB, MODES, LANES), F32)]
        + [pltpu.VMEM((MODES, 5, SUB, LANES), F32), pltpu.SemaphoreType.DMA((7,))],
        compiler_params=PARAMS,
        name="summary",
    )(*(pltpu.with_memory_space_constraint(x, pltpu.HBM) for x in sources))
    got = exchange(msg, near)
    natural = jax.ShapeDtypeStruct(queries.shape, F32)
    units = jax.ShapeDtypeStruct((MODES, HALF, LANES), F32)
    local = (natural, natural, units, units, units)
    local = local + (jax.ShapeDtypeStruct((4, MODES, LANES), F32),)
    msg, enter, *early = pl.pallas_call(
        middle_kernel,
        out_shape=(MESSAGE, jax.ShapeDtypeStruct((MODES, LANES), F32)) + local,
        in_specs=[VMEM] * 3,
        out_specs=(VMEM,) * 8,
        scratch_shapes=[stepped],
        compiler_params=PARAMS,
        name="middle",
    )(got, near_table, pack)
    got = exchange(msg, far)
    grad_q, grad_k, grad_v, grad_res, grad_skip = pl.pallas_call(
        final_kernel,
        out_shape=(
            wide,
            wide,
            wide,
            jax.ShapeDtypeStruct((MODES, HALF), F32),
            jax.ShapeDtypeStruct((1, HALF), F32),
        ),
        in_specs=[VMEM] * 12,
        out_specs=(ANY,) * 5,
        scratch_shapes=[held] * 3
        + [small, pltpu.VMEM((1, HALF), F32), pltpu.VMEM((LANES, LANES), F32)]
        + [pltpu.VMEM((2, TALL, queries.shape[1]), F32)]
        + [pltpu.SemaphoreType.DMA((2,)), pltpu.SemaphoreType.DMA((3, HALF // TALL))]
        + [pltpu.VMEM(x.shape, F32) for x in local]
        + [stepped],
        compiler_params=PARAMS,
        name="final",
    )(got, enter, pack, *early, keys, values, grad_out)
    return (grad_q, grad_k, grad_v, grad_res.T, grad_skip.reshape(HALF))


def solution(mesh):
    in_specs = (
        P("tp", "ctx"),
        P("tp", "ctx"),
        P("tp", "ctx"),
        P("tp", "ctx"),
        P("tp", None),
        P("tp", None),
        P("tp"),
    )
    out_specs = (P("tp", "ctx"), P("tp", "ctx"), P("tp", "ctx"), P("tp", None), P("tp"))
    return jax.shard_map(shards, mesh=mesh, in_specs=in_specs, out_specs=out_specs, check_vma=False)
```

```python
import math

import jax
import jax.numpy as jnp
from jax import lax
from jax.experimental import pallas as pl
from jax.experimental.pallas import tpu as pltpu
from jax.sharding import PartitionSpec as P

MODES = 16
LANES = 128
SUB = 8
HALF = 64
STEPS = 64
PITCH = STEPS + 1
CHUNKS = 16
LOCAL = STEPS * CHUNKS
GROUP = 8
EARLY = 4
NEAR_ORDER = tuple((k + 5) % GROUP for k in range(GROUP))
FAR_ORDER = (5, 7, 6, 4, 3, 2, 1, 0)
PARTS = 2
TALL = 16
UNITS = 0
SIGNAL = UNITS + PITCH * SUB
FORWARD = SIGNAL + PITCH * SUB
BACKWARD = FORWARD + MODES * SUB
RATES = BACKWARD + MODES * SUB
GAINS = RATES + MODES
WEIGHTS = GAINS + MODES
SKIPS = WEIGHTS + MODES
PACK = SKIPS + SUB
SUMS = MODES
DIRECT = SUMS + MODES // 2
ROWS = DIRECT + 1
F32 = jnp.float32
NORM = 1.0 / math.sqrt(65536)


def iota(shape, dim):
    return lax.broadcasted_iota(jnp.int32, shape, dim)


def twice(rows):
    return jnp.concatenate([rows, rows], axis=1)


def lift(rows, m):
    return jnp.broadcast_to(rows[m : m + 1], (SUB, LANES))


def to_steps(x, out_ref, base):
    for p in range(4):
        low = x[:, p * LANES : (p + 1) * LANES]
        high = x[:, (p + 4) * LANES : (p + 5) * LANES]
        turned = jnp.concatenate([low, high], axis=0).T
        for q in range(2):
            first = base + (2 * p + q) * PITCH
            out_ref[first : first + STEPS, :] = turned[q * STEPS : (q + 1) * STEPS]


def from_steps(ref, out_ref):
    for p in range(4):
        first = 2 * p * PITCH
        parts = [ref[first : first + STEPS, :], ref[first + PITCH : first + PITCH + STEPS, :]]
        turned = jnp.concatenate(parts, axis=0).T
        out_ref[:, p * LANES : (p + 1) * LANES] = turned[:HALF]
        out_ref[:, (p + 4) * LANES : (p + 5) * LANES] = turned[HALF:]


def turned_rows(rows):
    return jnp.concatenate([rows, jnp.zeros((LANES - MODES, LANES), F32)], axis=0).T


def step_rows(step):
    return pl.ds(step, SUB, stride=PITCH)


def packed_modes(table):
    upper = iota((SUB, LANES), 1) >= HALF
    return jnp.where(upper, table[SUB:], table[:SUB])


def write_message(msg_ref, states, sums, direct):
    for j in range(GROUP):
        first = j * ROWS
        msg_ref[first : first + MODES] = states
        msg_ref[first + SUMS : first + DIRECT] = sums
        msg_ref[first + DIRECT : first + ROWS] = direct


def one_minus_exp(x):
    series = jnp.ones_like(x)
    for n in range(9, 1, -1):
        series = 1.0 - series * (x * (1.0 / n))
    return jnp.where(x < 0.25, x * series, 1.0 - jnp.exp(-x))


def total_of(terms):
    total = terms[0]
    for term in terms[1:]:
        total = total + term
    return total


def added(terms):
    while len(terms) > 1:
        terms = [a + b for a, b in zip(terms[::2], terms[1::2])]
    return terms[0]


def summary_kernel(
    q_any, k_any, v_any, g_any, rate_any, residue_any, skip_any,
    pack_ref, msg_ref, near_ref,
    q_ref, k_ref, v_ref, g_ref, rate_ref, residue_ref, skip_ref,
    row_ref, decay_ref, sems,
):
    small = ((rate_any, rate_ref), (residue_any, residue_ref), (skip_any, skip_ref))
    copies = [pltpu.make_async_copy(a, b, sems.at[n]) for n, (a, b) in enumerate(small)]
    large = ((k_any, k_ref), (v_any, v_ref), (g_any, g_ref), (q_any, q_ref))
    for n, (a, b) in enumerate(large):
        for part in range(PARTS):
            rows = pl.ds(part * (HALF // PARTS), HALF // PARTS)
            sem = sems.at[len(small) + n * PARTS + part]
            copies.append(pltpu.make_async_copy(a.at[rows, :], b.at[rows, :], sem))
    for copy in copies:
        copy.start()

    for copy in copies[: len(small)]:
        copy.wait()
    copies = copies[len(small) :]
    rates = twice(rate_ref[...])
    gains = jnp.sqrt(one_minus_exp(2.0 * rates))
    skips = jnp.concatenate([skip_ref[...], skip_ref[...]], axis=1)
    pack_ref[RATES : RATES + MODES] = rates
    pack_ref[GAINS : GAINS + MODES] = gains
    pack_ref[WEIGHTS : WEIGHTS + MODES] = twice(residue_ref[...]) * gains
    pack_ref[SKIPS : SKIPS + SUB] = jnp.broadcast_to(skips, (SUB, LANES))
    row_ref[0] = jnp.exp(-rates)
    near_ref[0] = jnp.exp(-rates)
    near_ref[1] = jnp.exp(-float(LOCAL) * rates)
    row_ref[1] = jnp.exp(-float(STEPS * SUB) * rates)
    for i in range(STEPS // SUB):
        row_ref[2 + i] = jnp.exp(-float(SUB * i) * rates)
    row = iota((SUB, LANES), 0)
    upper = iota((SUB, LANES), 1) >= HALF
    row_f = row.astype(F32)
    chunk = jnp.where(upper, row_f + SUB, row_f)
    for m in range(MODES):
        r = pack_ref[RATES + m : RATES + m + 1, :]
        for n, d in enumerate((1, 2, 4)):
            decay_ref[m, n] = jnp.where(row >= d, jnp.exp(-float(STEPS * d) * r), 0.0)
        decay_ref[m, 3] = jnp.where(upper, jnp.exp(-(STEPS * row_f) * r), 0.0)
        decay_ref[m, 4] = jnp.exp(-(STEPS * chunk) * r)

    for copy in copies[: 2 * PARTS]:
        copy.wait()
    to_steps(k_ref[...].astype(F32) * v_ref[...].astype(F32), pack_ref, UNITS)
    for copy in copies[2 * PARTS :]:
        copy.wait()
    to_steps(g_ref[...].astype(F32) * q_ref[...].astype(F32), pack_ref, SIGNAL)

    zero = jnp.zeros((SUB, LANES), F32)
    ends, adjoints, totals = [], [], []
    lags = [zero] * SUB
    for half in range(2):
        modes = range(half * 8, half * 8 + 8)
        factor = [jnp.exp(-lift(pack_ref, RATES + m)) for m in modes]

        def body(i, carry):
            state, total, back, lags = carry
            u = [pack_ref[step_rows(UNITS + i * SUB + t), :] for t in range(SUB)]
            s = [pack_ref[step_rows(SIGNAL + i * SUB + t), :] for t in range(SUB)]
            part = [s[SUB - 1]] * 8
            for t in reversed(range(SUB - 1)):
                part = [f * p + s[t] for f, p in zip(factor, part)]
            total = [t + x * p for t, x, p in zip(total, state, part)]
            power = [row_ref[2 + i, m : m + 1, :] for m in modes]
            back = [b + w * p for b, w, p in zip(back, power, part)]
            for t in range(SUB):
                state = [f * x + u[t] for f, x in zip(factor, state)]
            if half == 0:
                lags = [
                    lags[d] + total_of([s[t] * u[t - d] for t in range(d, SUB)])
                    for d in range(SUB)
                ]
            return state, total, back, lags

        carry = ([zero] * 8, [zero] * 8, [zero] * 8, lags if half == 0 else [])
        state, total, back, found = lax.fori_loop(0, STEPS // SUB, body, carry, unroll=2)
        if half == 0:
            lags = found
        for n, m in enumerate(modes):
            within = lags[SUB - 1]
            for d in reversed(range(SUB - 1)):
                within = factor[n] * within + lags[d]
            scan = state[n]
            for j, d in enumerate((1, 2, 4)):
                scan = scan + decay_ref[m, j] * pltpu.roll(scan, d, 0)
            last = scan[SUB - 1 : SUB]
            last_other = pltpu.roll(last, HALF, 1)
            start = jnp.where(row >= 1, pltpu.roll(scan, 1, 0), 0.0)
            start = start + decay_ref[m, 3] * last_other
            pack_ref[FORWARD + m * SUB : FORWARD + (m + 1) * SUB] = start
            pack_ref[BACKWARD + m * SUB : BACKWARD + (m + 1) * SUB] = back[n]
            ends.append(last + row_ref[1, m : m + 1, :] * last_other)
            adjoints.append(jnp.sum(decay_ref[m, 4] * back[n], axis=0, keepdims=True))
            cross = factor[n] * (total[n] + start * back[n])
            totals.append(jnp.sum(within + cross, axis=0, keepdims=True))
    ends = jnp.concatenate(ends, axis=0)
    adjoints = jnp.concatenate(adjoints, axis=0)
    totals = jnp.concatenate(totals, axis=0)
    direct = jnp.sum(lags[0], axis=0, keepdims=True)
    adjoints = adjoints + pltpu.roll(adjoints, HALF, 1)
    totals = totals + pltpu.roll(totals, HALF, 1)
    direct = direct + pltpu.roll(direct, HALF, 1)
    lanes_up = iota((MODES, LANES), 1) >= HALF
    write_message(
        msg_ref, jnp.where(lanes_up, ends, adjoints), packed_modes(totals), direct
    )


def local_outputs(
    pack_ref,
    mixed_ref, back_ref, after_ref, before_ref, block_ref, table_ref,
    steps_ref,
):
    rates = pack_ref[RATES : RATES + MODES]
    skip = pack_ref[SKIPS : SKIPS + SUB]
    wide = [lift(rates, m) for m in range(MODES)]
    factor = [jnp.exp(-r) for r in wide]
    weight = [lift(pack_ref, WEIGHTS + m) for m in range(MODES)]

    def run(source, dst_ref, start, flip):
        def body(i, state):
            step = STEPS - 1 - i if flip else i
            x = pack_ref[step_rows(source + step), :]
            state = [f * z + x for f, z in zip(factor, state)]
            dst_ref[step_rows(step), :] = (
                added([w * z for w, z in zip(weight, state)]) + skip * x
            )
            return state

        lax.fori_loop(0, STEPS, body, start, unroll=8)

    row = iota((SUB, LANES), 0)
    upper = iota((SUB, LANES), 1) >= HALF
    run(
        UNITS, steps_ref,
        [pack_ref[FORWARD + m * SUB : FORWARD + (m + 1) * SUB] for m in range(MODES)], False,
    )
    from_steps(steps_ref, mixed_ref)
    start_b = []
    for m in range(MODES):
        scan = pack_ref[BACKWARD + m * SUB : BACKWARD + (m + 1) * SUB]
        for d in (1, 2, 4):
            decay = jnp.where(row < SUB - d, jnp.exp(-float(STEPS * d) * wide[m]), 0.0)
            scan = scan + decay * pltpu.roll(scan, SUB - d, 0)
        first_other = pltpu.roll(lift(scan, 0), HALF, 1)
        start = jnp.where(row < SUB - 1, pltpu.roll(scan, SUB - 1, 0), 0.0)
        decay = jnp.exp(-(STEPS * (SUB - 1 - row).astype(F32)) * wide[m])
        start_b.append(start + jnp.where(upper, 0.0, decay * first_other))
    run(SIGNAL, steps_ref, start_b, True)
    from_steps(steps_ref, back_ref)

    rate_cols = turned_rows(rates)
    weight_cols = turned_rows(pack_ref[WEIGHTS : WEIGHTS + MODES])
    token = iota((HALF, LANES), 1).astype(F32)
    for m in range(MODES):
        r = jnp.broadcast_to(rate_cols[:HALF, m : m + 1], (HALF, LANES))
        w = jnp.broadcast_to(weight_cols[:HALF, m : m + 1], (HALF, LANES))
        after_ref[m] = w * jnp.exp(-(token + 1.0) * r)
        before_ref[m] = w * jnp.exp(-(LANES - token) * r)
        block_ref[m] = jnp.exp(-float(LANES) * r)
    lanes_up = iota((MODES, LANES), 1) >= HALF
    place = lax.rem(lax.axis_index("ctx"), GROUP)
    ahead = jnp.where(lanes_up, place, GROUP - 1 - place).astype(F32)
    table_ref[0] = jnp.exp(-rates)
    table_ref[1] = jnp.exp(-float(LOCAL * GROUP) * rates)
    table_ref[2] = jnp.exp(-(LOCAL * ahead) * rates)
    table_ref[3] = pack_ref[GAINS : GAINS + MODES] * NORM


def combine(got_ref, order, factor, rho, place):
    lanes_up = iota((MODES, LANES), 1) >= HALF
    zero = jnp.zeros((MODES, LANES), F32)
    firsts = [order.index(k) * ROWS for k in range(GROUP)]
    pairs = [got_ref[f : f + MODES] for f in firsts]
    fwd, bwd = zero, zero
    enter_f, enter_b = zero, zero
    cross = zero
    sums = jnp.zeros((SUB, LANES), F32)
    direct = jnp.zeros((1, LANES), F32)
    for k in range(GROUP):
        enter_f = jnp.where(place == k, fwd, enter_f)
        cross = cross + fwd * pltpu.roll(pairs[k], HALF, 1)
        fwd = rho * fwd + pairs[k]
        sums = sums + got_ref[firsts[k] + SUMS : firsts[k] + DIRECT]
        direct = direct + got_ref[firsts[k] + DIRECT : firsts[k] + ROWS]
    for k in reversed(range(GROUP)):
        enter_b = jnp.where(place == k, bwd, enter_b)
        bwd = rho * bwd + pairs[k]
    entering = jnp.where(lanes_up, enter_f, enter_b)
    joint = jnp.where(lanes_up, fwd, bwd)
    cross = factor * cross
    cross = jnp.where(lanes_up, cross, pltpu.roll(cross, HALF, 1))
    return joint, sums + packed_modes(cross), direct, entering


def starts_early():
    return lax.div(lax.axis_index("ctx"), GROUP) < EARLY


def first_plane():
    return lax.div(lax.axis_index("ctx"), GROUP) == 0


def one_way(rows, unit_ref, block_ref, local_ref, enter, blocks, full_ref, half):
    parts = [unit_ref[m, rows, :] * enter[:, m : m + 1] for m in range(MODES)]
    for n, b in enumerate(blocks):
        cols = slice(b * LANES, (b + 1) * LANES)
        full_ref[half * SUB : (half + 1) * SUB, cols] = local_ref[rows, cols] + added(parts)
        if n < len(blocks) - 1:
            parts = [x * block_ref[m, rows, :] for m, x in enumerate(parts)]


def halves(i):
    for half in range(2):
        yield half, pl.multiple_of(i * TALL + half * SUB, SUB)


def add_forward(i, enter_cols, mixed_ref, after_ref, block_ref, g_ref, gq_ref, full_ref):
    for half, first in halves(i):
        rows = pl.ds(first, SUB)
        enter = enter_cols[pl.ds(HALF + first, SUB), :]
        one_way(rows, after_ref, block_ref, mixed_ref, enter, range(8), full_ref, half)
    rows = pl.ds(pl.multiple_of(i * TALL, TALL), TALL)
    for b in range(8):
        cols = slice(b * LANES, (b + 1) * LANES)
        mixed = full_ref[:, cols]
        gq_ref[rows, cols] = (g_ref[rows, cols].astype(F32) * mixed).astype(jnp.bfloat16)


def add_backward(
    i, enter_cols, back_ref, before_ref, block_ref, k_ref, v_ref, gk_ref, gv_ref, full_ref
):
    for half, first in halves(i):
        rows = pl.ds(first, SUB)
        enter = enter_cols[rows, :]
        one_way(rows, before_ref, block_ref, back_ref, enter, range(7, -1, -1), full_ref, half)
    rows = pl.ds(pl.multiple_of(i * TALL, TALL), TALL)
    for b in range(8):
        cols = slice(b * LANES, (b + 1) * LANES)
        back = full_ref[:, cols]
        gk_ref[rows, cols] = (v_ref[rows, cols].astype(F32) * back).astype(jnp.bfloat16)
        gv_ref[rows, cols] = (k_ref[rows, cols].astype(F32) * back).astype(jnp.bfloat16)


def middle_kernel(got_ref, near_ref, pack_ref, g_ref, msg_ref, enter_ref, *refs):
    local, gq_ref, (steps_ref, enter_cols, full_ref) = refs[:6], refs[6], refs[7:]
    joint, sums, direct, entering = combine(
        got_ref, NEAR_ORDER, near_ref[0], near_ref[1], lax.rem(lax.axis_index("ctx"), GROUP)
    )
    enter_ref[...] = entering
    write_message(msg_ref, joint, sums, direct)

    @pl.when(starts_early())
    def _():
        local_outputs(pack_ref, *local, steps_ref)

    @pl.when(first_plane())
    def _():
        mixed_ref, _, after_ref, _, block_ref, _ = local
        enter_cols[...] = turned_rows(entering)

        def body(i, carry):
            add_forward(
                i, enter_cols, mixed_ref, after_ref, block_ref, g_ref, gq_ref, full_ref
            )
            return carry

        lax.fori_loop(0, HALF // TALL, body, 0, unroll=2)


def final_kernel(*refs):
    got, enter, pack, *early = refs[:9]
    ready, rest, late, steps = refs[9], refs[10:-7], refs[-7:-1], refs[-1]

    @pl.when(first_plane())
    def _():
        finish(got, enter, *early, ready, *rest)

    @pl.when(jnp.logical_and(starts_early(), jnp.logical_not(first_plane())))
    def _():
        finish(got, enter, *early, None, *rest)

    @pl.when(jnp.logical_not(starts_early()))
    def _():
        local_outputs(pack, *late, steps)
        finish(got, enter, *late, None, *rest)


def finish(
    got_ref, enter_ref, mixed_ref, back_ref, after_ref, before_ref, block_ref, table_ref,
    ready_ref, k_ref, v_ref, g_ref,
    gq_any, gk_any, gv_any, gr_any, gs_any,
    gq_ref, gk_ref, gv_ref, gr_ref, gs_ref, enter_cols, full_ref, sems, out_sems,
):
    copies = []
    if ready_ref is not None:
        copies.append(pltpu.make_async_copy(ready_ref, gq_any, sems.at[2]))
        copies[0].start()
    joint, sums, direct, outer = combine(
        got_ref, FAR_ORDER, table_ref[0], table_ref[1], lax.div(lax.axis_index("ctx"), GROUP)
    )
    enter_cols[...] = turned_rows(enter_ref[...] + table_ref[2] * outer)
    scaled = sums * packed_modes(table_ref[3])
    gr_ref[0:SUB] = scaled[:, :HALF]
    gr_ref[SUB:MODES] = scaled[:, HALF:]
    gs_ref[...] = direct[:, :HALF] * NORM
    small = [
        pltpu.make_async_copy(gr_ref, gr_any, sems.at[0]),
        pltpu.make_async_copy(gs_ref, gs_any, sems.at[1]),
    ]
    for copy in small:
        copy.start()
    copies.extend(small)

    def out_copies(i):
        rows = pl.ds(pl.multiple_of(i * TALL, TALL), TALL)
        pairs = ((gk_ref, gk_any), (gv_ref, gv_any))
        if ready_ref is None:
            pairs += ((gq_ref, gq_any),)
        return [
            pltpu.make_async_copy(a.at[rows, :], b.at[rows, :], out_sems.at[n, i])
            for n, (a, b) in enumerate(pairs)
        ]

    def body(i, carry):
        if ready_ref is None:
            add_forward(
                i, enter_cols, mixed_ref, after_ref, block_ref, g_ref, gq_ref, full_ref.at[0]
            )
        add_backward(
            i, enter_cols, back_ref, before_ref, block_ref,
            k_ref, v_ref, gk_ref, gv_ref, full_ref.at[1],
        )
        for copy in out_copies(i):
            copy.start()
        return carry

    lax.fori_loop(0, HALF // TALL, body, 0, unroll=4)
    for i in range(HALF // TALL):
        copies.extend(out_copies(i))
    for copy in copies:
        copy.wait()


VMEM = pl.BlockSpec(memory_space=pltpu.VMEM)
ANY = pl.BlockSpec(memory_space=pl.ANY)
PARAMS = pltpu.CompilerParams(vmem_limit_bytes=32 * 1024 * 1024)
MESSAGE = jax.ShapeDtypeStruct((GROUP * ROWS, LANES), F32)


def exchange(msg, groups):
    rows = msg.reshape(GROUP * ROWS, 1, LANES)
    rows = lax.all_to_all(rows, "ctx", 0, 0, axis_index_groups=groups, tiled=True)
    return rows.reshape(GROUP * ROWS, LANES)


def shards(queries, keys, values, grad_out, residues, decay_rate, skip_gain):
    near = [[z * GROUP + k for k in NEAR_ORDER] for z in range(GROUP)]
    far = [[z * GROUP + k for z in FAR_ORDER] for k in range(GROUP)]
    wide = jax.ShapeDtypeStruct(queries.shape, jnp.bfloat16)
    held = pltpu.VMEM(queries.shape, jnp.bfloat16)

    stepped = pltpu.VMEM((PITCH * SUB, LANES), F32)
    small = pltpu.VMEM((MODES, HALF), F32)
    packed = jax.ShapeDtypeStruct((PACK, LANES), F32)
    sources = (
        queries, keys, values, grad_out,
        decay_rate.T, residues.T, skip_gain.reshape(1, HALF),
    )
    pack, msg, near_table = pl.pallas_call(
        summary_kernel,
        out_shape=(packed, MESSAGE, jax.ShapeDtypeStruct((2, MODES, LANES), F32)),
        in_specs=[ANY] * 7,
        out_specs=(VMEM,) * 3,
        scratch_shapes=[held] * 4
        + [small, small, pltpu.VMEM((1, HALF), F32)]
        + [pltpu.VMEM((2 + STEPS // SUB, MODES, LANES), F32)]
        + [pltpu.VMEM((MODES, 5, SUB, LANES), F32), pltpu.SemaphoreType.DMA((3 + 4 * PARTS,))],
        compiler_params=PARAMS,
        name="summary",
    )(*(pltpu.with_memory_space_constraint(x, pltpu.HBM) for x in sources))
    got = exchange(msg, near)
    natural = jax.ShapeDtypeStruct(queries.shape, F32)
    units = jax.ShapeDtypeStruct((MODES, HALF, LANES), F32)
    local = (natural, natural, units, units, units)
    local = local + (jax.ShapeDtypeStruct((4, MODES, LANES), F32),)
    msg, enter, *early, ready = pl.pallas_call(
        middle_kernel,
        out_shape=(MESSAGE, jax.ShapeDtypeStruct((MODES, LANES), F32)) + local + (wide,),
        in_specs=[VMEM] * 4,
        out_specs=(VMEM,) * 9,
        scratch_shapes=[stepped, pltpu.VMEM((LANES, LANES), F32)]
        + [pltpu.VMEM((TALL, queries.shape[1]), F32)],
        compiler_params=PARAMS,
        name="middle",
    )(got, near_table, pack, grad_out)
    got = exchange(msg, far)
    grad_q, grad_k, grad_v, grad_res, grad_skip = pl.pallas_call(
        final_kernel,
        out_shape=(
            wide,
            wide,
            wide,
            jax.ShapeDtypeStruct((MODES, HALF), F32),
            jax.ShapeDtypeStruct((1, HALF), F32),
        ),
        in_specs=[VMEM] * 13,
        out_specs=(ANY,) * 5,
        scratch_shapes=[held] * 3
        + [small, pltpu.VMEM((1, HALF), F32), pltpu.VMEM((LANES, LANES), F32)]
        + [pltpu.VMEM((2, TALL, queries.shape[1]), F32)]
        + [pltpu.SemaphoreType.DMA((3,)), pltpu.SemaphoreType.DMA((3, HALF // TALL))]
        + [pltpu.VMEM(x.shape, F32) for x in local]
        + [stepped],
        compiler_params=PARAMS,
        name="final",
    )(got, enter, pack, *early, ready, keys, values, grad_out)
    return (grad_q, grad_k, grad_v, grad_res.T, grad_skip.reshape(HALF))


def solution(mesh):
    in_specs = (
        P("tp", "ctx"),
        P("tp", "ctx"),
        P("tp", "ctx"),
        P("tp", "ctx"),
        P("tp", None),
        P("tp", None),
        P("tp"),
    )
    out_specs = (P("tp", "ctx"), P("tp", "ctx"), P("tp", "ctx"), P("tp", None), P("tp"))
    return jax.shard_map(shards, mesh=mesh, in_specs=in_specs, out_specs=out_specs, check_vma=False)
```

```python
import math

import jax
import jax.numpy as jnp
from jax import lax
from jax.experimental import pallas as pl
from jax.experimental.pallas import tpu as pltpu
from jax.sharding import PartitionSpec as P

MODES = 16
LANES = 128
SUB = 8
HALF = 64
STEPS = 64
PITCH = STEPS + 1
CHUNKS = 16
LOCAL = STEPS * CHUNKS
GROUP = 8
EARLY = 4
NEAR_ORDER = tuple((k + 5) % GROUP for k in range(GROUP))
FAR_ORDER = (5, 7, 6, 4, 3, 2, 1, 0)
PARTS = 2
TALL = 16
UNITS = 0
SIGNAL = UNITS + PITCH * SUB
FORWARD = SIGNAL + PITCH * SUB
BACKWARD = FORWARD + MODES * SUB
RATES = BACKWARD + MODES * SUB
GAINS = RATES + MODES
WEIGHTS = GAINS + MODES
SKIPS = WEIGHTS + MODES
PACK = SKIPS + SUB
SUMS = MODES
DIRECT = SUMS + MODES // 2
ROWS = DIRECT + 1
F32 = jnp.float32
NORM = 1.0 / math.sqrt(65536)


def iota(shape, dim):
    return lax.broadcasted_iota(jnp.int32, shape, dim)


def twice(rows):
    return jnp.concatenate([rows, rows], axis=1)


def lift(rows, m):
    return jnp.broadcast_to(rows[m : m + 1], (SUB, LANES))


def to_steps(x, out_ref, base):
    for p in range(4):
        low = x[:, p * LANES : (p + 1) * LANES]
        high = x[:, (p + 4) * LANES : (p + 5) * LANES]
        turned = jnp.concatenate([low, high], axis=0).T
        for q in range(2):
            first = base + (2 * p + q) * PITCH
            out_ref[first : first + STEPS, :] = turned[q * STEPS : (q + 1) * STEPS]


def from_steps(ref, out_ref):
    for p in range(4):
        first = 2 * p * PITCH
        parts = [ref[first : first + STEPS, :], ref[first + PITCH : first + PITCH + STEPS, :]]
        turned = jnp.concatenate(parts, axis=0).T
        out_ref[:, p * LANES : (p + 1) * LANES] = turned[:HALF]
        out_ref[:, (p + 4) * LANES : (p + 5) * LANES] = turned[HALF:]


def turned_rows(rows):
    return jnp.concatenate([rows, jnp.zeros((LANES - MODES, LANES), F32)], axis=0).T


def step_rows(step):
    return pl.ds(step, SUB, stride=PITCH)


def packed_modes(table):
    upper = iota((SUB, LANES), 1) >= HALF
    return jnp.where(upper, table[SUB:], table[:SUB])


def write_message(msg_ref, states, sums, direct):
    for j in range(GROUP):
        first = j * ROWS
        msg_ref[first : first + MODES] = states
        msg_ref[first + SUMS : first + DIRECT] = sums
        msg_ref[first + DIRECT : first + ROWS] = direct


def one_minus_exp(x):
    series = jnp.ones_like(x)
    for n in range(9, 1, -1):
        series = 1.0 - series * (x * (1.0 / n))
    return jnp.where(x < 0.25, x * series, 1.0 - jnp.exp(-x))


def total_of(terms):
    total = terms[0]
    for term in terms[1:]:
        total = total + term
    return total


def added(terms):
    while len(terms) > 1:
        terms = [a + b for a, b in zip(terms[::2], terms[1::2])]
    return terms[0]


def summary_kernel(
    q_any, k_any, v_any, g_any, rate_any, residue_any, skip_any,
    pack_ref, msg_ref, near_ref,
    q_ref, k_ref, v_ref, g_ref, rate_ref, residue_ref, skip_ref,
    row_ref, decay_ref, sems,
):
    small = ((rate_any, rate_ref), (residue_any, residue_ref), (skip_any, skip_ref))
    copies = [pltpu.make_async_copy(a, b, sems.at[n]) for n, (a, b) in enumerate(small)]
    large = ((k_any, k_ref), (v_any, v_ref), (g_any, g_ref), (q_any, q_ref))
    for n, (a, b) in enumerate(large):
        for part in range(PARTS):
            rows = pl.ds(part * (HALF // PARTS), HALF // PARTS)
            sem = sems.at[len(small) + n * PARTS + part]
            copies.append(pltpu.make_async_copy(a.at[rows, :], b.at[rows, :], sem))
    for copy in copies:
        copy.start()

    for copy in copies[: len(small)]:
        copy.wait()
    copies = copies[len(small) :]
    rates = twice(rate_ref[...])
    gains = jnp.sqrt(one_minus_exp(2.0 * rates))
    skips = jnp.concatenate([skip_ref[...], skip_ref[...]], axis=1)
    pack_ref[RATES : RATES + MODES] = rates
    pack_ref[GAINS : GAINS + MODES] = gains
    pack_ref[WEIGHTS : WEIGHTS + MODES] = twice(residue_ref[...]) * gains
    pack_ref[SKIPS : SKIPS + SUB] = jnp.broadcast_to(skips, (SUB, LANES))
    row_ref[0] = jnp.exp(-rates)
    near_ref[0] = jnp.exp(-rates)
    near_ref[1] = jnp.exp(-float(LOCAL) * rates)
    row_ref[1] = jnp.exp(-float(STEPS * SUB) * rates)
    for i in range(STEPS // SUB):
        row_ref[2 + i] = jnp.exp(-float(SUB * i) * rates)
    row = iota((SUB, LANES), 0)
    upper = iota((SUB, LANES), 1) >= HALF
    row_f = row.astype(F32)
    chunk = jnp.where(upper, row_f + SUB, row_f)
    for m in range(MODES):
        r = pack_ref[RATES + m : RATES + m + 1, :]
        for n, d in enumerate((1, 2, 4)):
            decay_ref[m, n] = jnp.where(row >= d, jnp.exp(-float(STEPS * d) * r), 0.0)
        decay_ref[m, 3] = jnp.where(upper, jnp.exp(-(STEPS * row_f) * r), 0.0)
        decay_ref[m, 4] = jnp.exp(-(STEPS * chunk) * r)

    for copy in copies[: 2 * PARTS]:
        copy.wait()
    to_steps(k_ref[...].astype(F32) * v_ref[...].astype(F32), pack_ref, UNITS)
    for copy in copies[2 * PARTS :]:
        copy.wait()
    to_steps(g_ref[...].astype(F32) * q_ref[...].astype(F32), pack_ref, SIGNAL)

    zero = jnp.zeros((SUB, LANES), F32)
    ends, adjoints, totals = [], [], []
    lags = [zero] * SUB
    for half in range(2):
        modes = range(half * 8, half * 8 + 8)
        factor = [jnp.exp(-lift(pack_ref, RATES + m)) for m in modes]

        def body(i, carry):
            state, total, back, lags = carry
            u = [pack_ref[step_rows(UNITS + i * SUB + t), :] for t in range(SUB)]
            s = [pack_ref[step_rows(SIGNAL + i * SUB + t), :] for t in range(SUB)]
            part = [s[SUB - 1]] * 8
            for t in reversed(range(SUB - 1)):
                part = [f * p + s[t] for f, p in zip(factor, part)]
            total = [t + x * p for t, x, p in zip(total, state, part)]
            power = [row_ref[2 + i, m : m + 1, :] for m in modes]
            back = [b + w * p for b, w, p in zip(back, power, part)]
            for t in range(SUB):
                state = [f * x + u[t] for f, x in zip(factor, state)]
            if half == 0:
                lags = [
                    lags[d] + total_of([s[t] * u[t - d] for t in range(d, SUB)])
                    for d in range(SUB)
                ]
            return state, total, back, lags

        carry = ([zero] * 8, [zero] * 8, [zero] * 8, lags if half == 0 else [])
        state, total, back, found = lax.fori_loop(0, STEPS // SUB, body, carry, unroll=2)
        if half == 0:
            lags = found
        for n, m in enumerate(modes):
            scan = state[n]
            for j, d in enumerate((1, 2, 4)):
                scan = scan + decay_ref[m, j] * pltpu.roll(scan, d, 0)
            last = scan[SUB - 1 : SUB]
            last_other = pltpu.roll(last, HALF, 1)
            start = jnp.where(row >= 1, pltpu.roll(scan, 1, 0), 0.0)
            start = start + decay_ref[m, 3] * last_other
            pack_ref[FORWARD + m * SUB : FORWARD + (m + 1) * SUB] = start
            pack_ref[BACKWARD + m * SUB : BACKWARD + (m + 1) * SUB] = back[n]
            ends.append(last + row_ref[1, m : m + 1, :] * last_other)
            adjoints.append(jnp.sum(decay_ref[m, 4] * back[n], axis=0, keepdims=True))
            totals.append(jnp.sum(total[n] + start * back[n], axis=0, keepdims=True))
    ends = jnp.concatenate(ends, axis=0)
    adjoints = jnp.concatenate(adjoints, axis=0)
    lags = [jnp.sum(x, axis=0, keepdims=True) for x in lags]
    direct = lags[0]
    within = jnp.broadcast_to(lags[SUB - 1], (MODES, LANES))
    for d in reversed(range(SUB - 1)):
        within = row_ref[0] * within + lags[d]
    totals = row_ref[0] * jnp.concatenate(totals, axis=0) + within
    adjoints = adjoints + pltpu.roll(adjoints, HALF, 1)
    totals = totals + pltpu.roll(totals, HALF, 1)
    direct = direct + pltpu.roll(direct, HALF, 1)
    lanes_up = iota((MODES, LANES), 1) >= HALF
    write_message(
        msg_ref, jnp.where(lanes_up, ends, adjoints), packed_modes(totals), direct
    )


def local_outputs(
    pack_ref,
    mixed_ref, back_ref, after_ref, before_ref, block_ref, table_ref,
    steps_ref,
):
    rates = pack_ref[RATES : RATES + MODES]
    skip = pack_ref[SKIPS : SKIPS + SUB]
    wide = [lift(rates, m) for m in range(MODES)]
    factor = [jnp.exp(-r) for r in wide]
    weight = [lift(pack_ref, WEIGHTS + m) for m in range(MODES)]

    def run(source, dst_ref, start, flip):
        def body(i, state):
            step = STEPS - 1 - i if flip else i
            x = pack_ref[step_rows(source + step), :]
            state = [f * z + x for f, z in zip(factor, state)]
            dst_ref[step_rows(step), :] = (
                added([w * z for w, z in zip(weight, state)]) + skip * x
            )
            return state

        lax.fori_loop(0, STEPS, body, start, unroll=8)

    row = iota((SUB, LANES), 0)
    upper = iota((SUB, LANES), 1) >= HALF
    run(
        UNITS, steps_ref,
        [pack_ref[FORWARD + m * SUB : FORWARD + (m + 1) * SUB] for m in range(MODES)], False,
    )
    from_steps(steps_ref, mixed_ref)
    start_b = []
    for m in range(MODES):
        scan = pack_ref[BACKWARD + m * SUB : BACKWARD + (m + 1) * SUB]
        for d in (1, 2, 4):
            decay = jnp.where(row < SUB - d, jnp.exp(-float(STEPS * d) * wide[m]), 0.0)
            scan = scan + decay * pltpu.roll(scan, SUB - d, 0)
        first_other = pltpu.roll(lift(scan, 0), HALF, 1)
        start = jnp.where(row < SUB - 1, pltpu.roll(scan, SUB - 1, 0), 0.0)
        decay = jnp.exp(-(STEPS * (SUB - 1 - row).astype(F32)) * wide[m])
        start_b.append(start + jnp.where(upper, 0.0, decay * first_other))
    run(SIGNAL, steps_ref, start_b, True)
    from_steps(steps_ref, back_ref)

    rate_cols = turned_rows(rates)
    weight_cols = turned_rows(pack_ref[WEIGHTS : WEIGHTS + MODES])
    token = iota((HALF, LANES), 1).astype(F32)
    for m in range(MODES):
        r = jnp.broadcast_to(rate_cols[:HALF, m : m + 1], (HALF, LANES))
        w = jnp.broadcast_to(weight_cols[:HALF, m : m + 1], (HALF, LANES))
        after_ref[m] = w * jnp.exp(-(token + 1.0) * r)
        before_ref[m] = w * jnp.exp(-(LANES - token) * r)
        block_ref[m] = jnp.exp(-float(LANES) * r)
    lanes_up = iota((MODES, LANES), 1) >= HALF
    place = lax.rem(lax.axis_index("ctx"), GROUP)
    ahead = jnp.where(lanes_up, place, GROUP - 1 - place).astype(F32)
    table_ref[0] = jnp.exp(-rates)
    table_ref[1] = jnp.exp(-float(LOCAL * GROUP) * rates)
    table_ref[2] = jnp.exp(-(LOCAL * ahead) * rates)
    table_ref[3] = pack_ref[GAINS : GAINS + MODES] * NORM


def combine(got_ref, order, factor, rho, place):
    lanes_up = iota((MODES, LANES), 1) >= HALF
    zero = jnp.zeros((MODES, LANES), F32)
    firsts = [order.index(k) * ROWS for k in range(GROUP)]
    pairs = [got_ref[f : f + MODES] for f in firsts]
    fwd, bwd = zero, zero
    enter_f, enter_b = zero, zero
    cross = zero
    sums = jnp.zeros((SUB, LANES), F32)
    direct = jnp.zeros((1, LANES), F32)
    for k in range(GROUP):
        enter_f = jnp.where(place == k, fwd, enter_f)
        cross = cross + fwd * pltpu.roll(pairs[k], HALF, 1)
        fwd = rho * fwd + pairs[k]
        sums = sums + got_ref[firsts[k] + SUMS : firsts[k] + DIRECT]
        direct = direct + got_ref[firsts[k] + DIRECT : firsts[k] + ROWS]
    for k in reversed(range(GROUP)):
        enter_b = jnp.where(place == k, bwd, enter_b)
        bwd = rho * bwd + pairs[k]
    entering = jnp.where(lanes_up, enter_f, enter_b)
    joint = jnp.where(lanes_up, fwd, bwd)
    cross = factor * cross
    cross = jnp.where(lanes_up, cross, pltpu.roll(cross, HALF, 1))
    return joint, sums + packed_modes(cross), direct, entering


def starts_early():
    return lax.div(lax.axis_index("ctx"), GROUP) < EARLY


def first_plane():
    return lax.div(lax.axis_index("ctx"), GROUP) == 0


def one_way(rows, unit_ref, block_ref, local_ref, enter, blocks, full_ref, half):
    parts = [unit_ref[m, rows, :] * enter[:, m : m + 1] for m in range(MODES)]
    for n, b in enumerate(blocks):
        cols = slice(b * LANES, (b + 1) * LANES)
        full_ref[half * SUB : (half + 1) * SUB, cols] = local_ref[rows, cols] + added(parts)
        if n < len(blocks) - 1:
            parts = [x * block_ref[m, rows, :] for m, x in enumerate(parts)]


def halves(i):
    for half in range(2):
        yield half, pl.multiple_of(i * TALL + half * SUB, SUB)


def add_forward(i, enter_cols, mixed_ref, after_ref, block_ref, g_ref, gq_ref, full_ref):
    for half, first in halves(i):
        rows = pl.ds(first, SUB)
        enter = enter_cols[pl.ds(HALF + first, SUB), :]
        one_way(rows, after_ref, block_ref, mixed_ref, enter, range(8), full_ref, half)
    rows = pl.ds(pl.multiple_of(i * TALL, TALL), TALL)
    for b in range(8):
        cols = slice(b * LANES, (b + 1) * LANES)
        mixed = full_ref[:, cols]
        gq_ref[rows, cols] = (g_ref[rows, cols].astype(F32) * mixed).astype(jnp.bfloat16)


def add_backward(
    i, enter_cols, back_ref, before_ref, block_ref, k_ref, v_ref, gk_ref, gv_ref, full_ref
):
    for half, first in halves(i):
        rows = pl.ds(first, SUB)
        enter = enter_cols[rows, :]
        one_way(rows, before_ref, block_ref, back_ref, enter, range(7, -1, -1), full_ref, half)
    rows = pl.ds(pl.multiple_of(i * TALL, TALL), TALL)
    for b in range(8):
        cols = slice(b * LANES, (b + 1) * LANES)
        back = full_ref[:, cols]
        gk_ref[rows, cols] = (v_ref[rows, cols].astype(F32) * back).astype(jnp.bfloat16)
        gv_ref[rows, cols] = (k_ref[rows, cols].astype(F32) * back).astype(jnp.bfloat16)


def middle_kernel(got_ref, near_ref, pack_ref, g_ref, msg_ref, enter_ref, *refs):
    local, gq_ref, (steps_ref, enter_cols, full_ref) = refs[:6], refs[6], refs[7:]
    joint, sums, direct, entering = combine(
        got_ref, NEAR_ORDER, near_ref[0], near_ref[1], lax.rem(lax.axis_index("ctx"), GROUP)
    )
    enter_ref[...] = entering
    write_message(msg_ref, joint, sums, direct)

    @pl.when(starts_early())
    def _():
        local_outputs(pack_ref, *local, steps_ref)

    @pl.when(first_plane())
    def _():
        mixed_ref, _, after_ref, _, block_ref, _ = local
        enter_cols[...] = turned_rows(entering)

        def body(i, carry):
            add_forward(
                i, enter_cols, mixed_ref, after_ref, block_ref, g_ref, gq_ref, full_ref
            )
            return carry

        lax.fori_loop(0, HALF // TALL, body, 0, unroll=2)


def final_kernel(*refs):
    got, enter, pack, *early = refs[:9]
    ready, rest, late, steps = refs[9], refs[10:-7], refs[-7:-1], refs[-1]

    @pl.when(first_plane())
    def _():
        finish(got, enter, *early, ready, *rest)

    @pl.when(jnp.logical_and(starts_early(), jnp.logical_not(first_plane())))
    def _():
        finish(got, enter, *early, None, *rest)

    @pl.when(jnp.logical_not(starts_early()))
    def _():
        local_outputs(pack, *late, steps)
        finish(got, enter, *late, None, *rest)


def finish(
    got_ref, enter_ref, mixed_ref, back_ref, after_ref, before_ref, block_ref, table_ref,
    ready_ref, k_ref, v_ref, g_ref,
    gq_any, gk_any, gv_any, gr_any, gs_any,
    gq_ref, gk_ref, gv_ref, gr_ref, gs_ref, enter_cols, full_ref, sems, out_sems,
):
    copies = []
    if ready_ref is not None:
        copies.append(pltpu.make_async_copy(ready_ref, gq_any, sems.at[2]))
        copies[0].start()
    joint, sums, direct, outer = combine(
        got_ref, FAR_ORDER, table_ref[0], table_ref[1], lax.div(lax.axis_index("ctx"), GROUP)
    )
    enter_cols[...] = turned_rows(enter_ref[...] + table_ref[2] * outer)
    scaled = sums * packed_modes(table_ref[3])
    gr_ref[0:SUB] = scaled[:, :HALF]
    gr_ref[SUB:MODES] = scaled[:, HALF:]
    gs_ref[...] = direct[:, :HALF] * NORM
    small = [
        pltpu.make_async_copy(gr_ref, gr_any, sems.at[0]),
        pltpu.make_async_copy(gs_ref, gs_any, sems.at[1]),
    ]
    for copy in small:
        copy.start()
    copies.extend(small)

    def out_copies(i):
        rows = pl.ds(pl.multiple_of(i * TALL, TALL), TALL)
        pairs = ((gk_ref, gk_any), (gv_ref, gv_any))
        if ready_ref is None:
            pairs += ((gq_ref, gq_any),)
        return [
            pltpu.make_async_copy(a.at[rows, :], b.at[rows, :], out_sems.at[n, i])
            for n, (a, b) in enumerate(pairs)
        ]

    def body(i, carry):
        if ready_ref is None:
            add_forward(
                i, enter_cols, mixed_ref, after_ref, block_ref, g_ref, gq_ref, full_ref.at[0]
            )
        add_backward(
            i, enter_cols, back_ref, before_ref, block_ref,
            k_ref, v_ref, gk_ref, gv_ref, full_ref.at[1],
        )
        for copy in out_copies(i):
            copy.start()
        return carry

    lax.fori_loop(0, HALF // TALL, body, 0, unroll=4)
    for i in range(HALF // TALL):
        copies.extend(out_copies(i))
    for copy in copies:
        copy.wait()


VMEM = pl.BlockSpec(memory_space=pltpu.VMEM)
ANY = pl.BlockSpec(memory_space=pl.ANY)
PARAMS = pltpu.CompilerParams(vmem_limit_bytes=32 * 1024 * 1024)
MESSAGE = jax.ShapeDtypeStruct((GROUP * ROWS, LANES), F32)


def exchange(msg, groups):
    rows = msg.reshape(GROUP * ROWS, 1, LANES)
    rows = lax.all_to_all(rows, "ctx", 0, 0, axis_index_groups=groups, tiled=True)
    return rows.reshape(GROUP * ROWS, LANES)


def shards(queries, keys, values, grad_out, residues, decay_rate, skip_gain):
    near = [[z * GROUP + k for k in NEAR_ORDER] for z in range(GROUP)]
    far = [[z * GROUP + k for z in FAR_ORDER] for k in range(GROUP)]
    wide = jax.ShapeDtypeStruct(queries.shape, jnp.bfloat16)
    held = pltpu.VMEM(queries.shape, jnp.bfloat16)

    stepped = pltpu.VMEM((PITCH * SUB + STEPS, LANES), F32)
    small = pltpu.VMEM((MODES, HALF), F32)
    packed = jax.ShapeDtypeStruct((PACK, LANES), F32)
    sources = (
        queries, keys, values, grad_out,
        decay_rate.T, residues.T, skip_gain.reshape(1, HALF),
    )
    pack, msg, near_table = pl.pallas_call(
        summary_kernel,
        out_shape=(packed, MESSAGE, jax.ShapeDtypeStruct((2, MODES, LANES), F32)),
        in_specs=[ANY] * 7,
        out_specs=(VMEM,) * 3,
        scratch_shapes=[held] * 4
        + [small, small, pltpu.VMEM((1, HALF), F32)]
        + [pltpu.VMEM((2 + STEPS // SUB, MODES, LANES), F32)]
        + [pltpu.VMEM((MODES, 5, SUB, LANES), F32), pltpu.SemaphoreType.DMA((3 + 4 * PARTS,))],
        compiler_params=PARAMS,
        name="summary",
    )(*(pltpu.with_memory_space_constraint(x, pltpu.HBM) for x in sources))
    got = exchange(msg, near)
    natural = jax.ShapeDtypeStruct(queries.shape, F32)
    units = jax.ShapeDtypeStruct((MODES, HALF, LANES), F32)
    local = (natural, natural, units, units, units)
    local = local + (jax.ShapeDtypeStruct((4, MODES, LANES), F32),)
    msg, enter, *early, ready = pl.pallas_call(
        middle_kernel,
        out_shape=(MESSAGE, jax.ShapeDtypeStruct((MODES, LANES), F32)) + local + (wide,),
        in_specs=[VMEM] * 4,
        out_specs=(VMEM,) * 9,
        scratch_shapes=[stepped, pltpu.VMEM((LANES, LANES), F32)]
        + [pltpu.VMEM((TALL, queries.shape[1]), F32)],
        compiler_params=PARAMS,
        name="middle",
    )(got, near_table, pack, grad_out)
    got = exchange(msg, far)
    grad_q, grad_k, grad_v, grad_res, grad_skip = pl.pallas_call(
        final_kernel,
        out_shape=(
            wide,
            wide,
            wide,
            jax.ShapeDtypeStruct((MODES, HALF), F32),
            jax.ShapeDtypeStruct((1, HALF), F32),
        ),
        in_specs=[VMEM] * 13,
        out_specs=(ANY,) * 5,
        scratch_shapes=[held] * 3
        + [small, pltpu.VMEM((1, HALF), F32), pltpu.VMEM((LANES, LANES), F32)]
        + [pltpu.VMEM((2, TALL, queries.shape[1]), F32)]
        + [pltpu.SemaphoreType.DMA((3,)), pltpu.SemaphoreType.DMA((3, HALF // TALL))]
        + [pltpu.VMEM(x.shape, F32) for x in local]
        + [stepped],
        compiler_params=PARAMS,
        name="final",
    )(got, enter, pack, *early, ready, keys, values, grad_out)
    return (grad_q, grad_k, grad_v, grad_res.T, grad_skip.reshape(HALF))


def solution(mesh):
    in_specs = (
        P("tp", "ctx"),
        P("tp", "ctx"),
        P("tp", "ctx"),
        P("tp", "ctx"),
        P("tp", None),
        P("tp", None),
        P("tp"),
    )
    out_specs = (P("tp", "ctx"), P("tp", "ctx"), P("tp", "ctx"), P("tp", None), P("tp"))
    return jax.shard_map(shards, mesh=mesh, in_specs=in_specs, out_specs=out_specs, check_vma=False)
```

```python
import math

import jax
import jax.numpy as jnp
from jax import lax
from jax.experimental import pallas as pl
from jax.experimental.pallas import tpu as pltpu
from jax.sharding import PartitionSpec as P

MODES = 16
LANES = 128
SUB = 8
HALF = 64
STEPS = 64
PITCH = STEPS + 1
CHUNKS = 16
LOCAL = STEPS * CHUNKS
GROUP = 8
EARLY = 4
NEAR_ORDER = tuple((k + 5) % GROUP for k in range(GROUP))
FAR_ORDER = (5, 7, 6, 4, 3, 2, 1, 0)
PARTS = 2
TALL = 16
UNITS = 0
SIGNAL = UNITS + PITCH * SUB
FORWARD = SIGNAL + PITCH * SUB
BACKWARD = FORWARD + MODES * SUB
RATES = BACKWARD + MODES * SUB
GAINS = RATES + MODES
WEIGHTS = GAINS + MODES
SKIPS = WEIGHTS + MODES
PACK = SKIPS + SUB
SUMS = MODES
DIRECT = SUMS + MODES // 2
ROWS = DIRECT + 1
F32 = jnp.float32
NORM = 1.0 / math.sqrt(65536)


def iota(shape, dim):
    return lax.broadcasted_iota(jnp.int32, shape, dim)


def twice(rows):
    return jnp.concatenate([rows, rows], axis=1)


def lift(rows, m):
    return jnp.broadcast_to(rows[m : m + 1], (SUB, LANES))


def to_steps(x, out_ref, base):
    for p in range(4):
        low = x[:, p * LANES : (p + 1) * LANES]
        high = x[:, (p + 4) * LANES : (p + 5) * LANES]
        turned = jnp.concatenate([low, high], axis=0).T
        for q in range(2):
            first = base + (2 * p + q) * PITCH
            out_ref[first : first + STEPS, :] = turned[q * STEPS : (q + 1) * STEPS]


def from_steps(ref, out_ref):
    for p in range(4):
        first = 2 * p * PITCH
        parts = [ref[first : first + STEPS, :], ref[first + PITCH : first + PITCH + STEPS, :]]
        turned = jnp.concatenate(parts, axis=0).T
        out_ref[:, p * LANES : (p + 1) * LANES] = turned[:HALF]
        out_ref[:, (p + 4) * LANES : (p + 5) * LANES] = turned[HALF:]


def turned_rows(rows):
    return jnp.concatenate([rows, jnp.zeros((LANES - MODES, LANES), F32)], axis=0).T


def step_rows(step):
    return pl.ds(step, SUB, stride=PITCH)


def packed_modes(table):
    upper = iota((SUB, LANES), 1) >= HALF
    return jnp.where(upper, table[SUB:], table[:SUB])


def write_message(msg_ref, states, sums, direct):
    for j in range(GROUP):
        first = j * ROWS
        msg_ref[first : first + MODES] = states
        msg_ref[first + SUMS : first + DIRECT] = sums
        msg_ref[first + DIRECT : first + ROWS] = direct


def one_minus_exp(x):
    series = jnp.ones_like(x)
    for n in range(9, 1, -1):
        series = 1.0 - series * (x * (1.0 / n))
    return jnp.where(x < 0.25, x * series, 1.0 - jnp.exp(-x))


def total_of(terms):
    total = terms[0]
    for term in terms[1:]:
        total = total + term
    return total


def added(terms):
    while len(terms) > 1:
        terms = [a + b for a, b in zip(terms[::2], terms[1::2])]
    return terms[0]


def summary_kernel(
    q_any, k_any, v_any, g_any, rate_any, residue_any, skip_any,
    pack_ref, msg_ref, near_ref,
    q_ref, k_ref, v_ref, g_ref, rate_ref, residue_ref, skip_ref,
    row_ref, decay_ref, sems,
):
    small = ((rate_any, rate_ref), (residue_any, residue_ref), (skip_any, skip_ref))
    copies = [pltpu.make_async_copy(a, b, sems.at[n]) for n, (a, b) in enumerate(small)]
    large = ((k_any, k_ref), (v_any, v_ref), (g_any, g_ref), (q_any, q_ref))
    for n, (a, b) in enumerate(large):
        for part in range(PARTS):
            rows = pl.ds(part * (HALF // PARTS), HALF // PARTS)
            sem = sems.at[len(small) + n * PARTS + part]
            copies.append(pltpu.make_async_copy(a.at[rows, :], b.at[rows, :], sem))
    for copy in copies:
        copy.start()

    for copy in copies[: len(small)]:
        copy.wait()
    copies = copies[len(small) :]
    rates = twice(rate_ref[...])
    gains = jnp.sqrt(one_minus_exp(2.0 * rates))
    skips = jnp.concatenate([skip_ref[...], skip_ref[...]], axis=1)
    pack_ref[RATES : RATES + MODES] = rates
    pack_ref[GAINS : GAINS + MODES] = gains
    pack_ref[WEIGHTS : WEIGHTS + MODES] = twice(residue_ref[...]) * gains
    pack_ref[SKIPS : SKIPS + SUB] = jnp.broadcast_to(skips, (SUB, LANES))
    row_ref[0] = jnp.exp(-rates)
    near_ref[0] = jnp.exp(-rates)
    near_ref[1] = jnp.exp(-float(LOCAL) * rates)
    row_ref[1] = jnp.exp(-float(STEPS * SUB) * rates)
    for i in range(STEPS // SUB):
        row_ref[2 + i] = jnp.exp(-float(SUB * i) * rates)
    row = iota((SUB, LANES), 0)
    upper = iota((SUB, LANES), 1) >= HALF
    row_f = row.astype(F32)
    chunk = jnp.where(upper, row_f + SUB, row_f)
    for m in range(MODES):
        r = pack_ref[RATES + m : RATES + m + 1, :]
        for n, d in enumerate((1, 2, 4)):
            decay_ref[m, n] = jnp.where(row >= d, jnp.exp(-float(STEPS * d) * r), 0.0)
        decay_ref[m, 3] = jnp.where(upper, jnp.exp(-(STEPS * row_f) * r), 0.0)
        decay_ref[m, 4] = jnp.exp(-(STEPS * chunk) * r)

    for copy in copies[: 2 * PARTS]:
        copy.wait()
    to_steps(k_ref[...].astype(F32) * v_ref[...].astype(F32), pack_ref, UNITS)
    for copy in copies[2 * PARTS :]:
        copy.wait()
    to_steps(g_ref[...].astype(F32) * q_ref[...].astype(F32), pack_ref, SIGNAL)

    zero = jnp.zeros((SUB, LANES), F32)
    ends, adjoints, totals = [], [], []
    lags = [zero] * SUB
    for half in range(2):
        modes = range(half * 8, half * 8 + 8)
        factor = [jnp.exp(-lift(pack_ref, RATES + m)) for m in modes]

        def body(i, carry):
            state, total, back, lags = carry
            u = [pack_ref[step_rows(UNITS + i * SUB + t), :] for t in range(SUB)]
            s = [pack_ref[step_rows(SIGNAL + i * SUB + t), :] for t in range(SUB)]
            part = [s[SUB - 1]] * 8
            for t in reversed(range(SUB - 1)):
                part = [f * p + s[t] for f, p in zip(factor, part)]
            total = [t + x * p for t, x, p in zip(total, state, part)]
            power = [row_ref[2 + i, m : m + 1, :] for m in modes]
            back = [b + w * p for b, w, p in zip(back, power, part)]
            for t in range(SUB):
                state = [f * x + u[t] for f, x in zip(factor, state)]
            if half == 0:
                lags = [
                    lags[d] + total_of([s[t] * u[t - d] for t in range(d, SUB)])
                    for d in range(SUB)
                ]
            return state, total, back, lags

        carry = ([zero] * 8, [zero] * 8, [zero] * 8, lags if half == 0 else [])
        state, total, back, found = lax.fori_loop(0, STEPS // SUB, body, carry, unroll=2)
        if half == 0:
            lags = found
        for n, m in enumerate(modes):
            scan = state[n]
            for j, d in enumerate((1, 2, 4)):
                scan = scan + decay_ref[m, j] * pltpu.roll(scan, d, 0)
            last = scan[SUB - 1 : SUB]
            last_other = pltpu.roll(last, HALF, 1)
            start = jnp.where(row >= 1, pltpu.roll(scan, 1, 0), 0.0)
            start = start + decay_ref[m, 3] * last_other
            pack_ref[FORWARD + m * SUB : FORWARD + (m + 1) * SUB] = start
            pack_ref[BACKWARD + m * SUB : BACKWARD + (m + 1) * SUB] = back[n]
            ends.append(last + row_ref[1, m : m + 1, :] * last_other)
            adjoints.append(jnp.sum(decay_ref[m, 4] * back[n], axis=0, keepdims=True))
            totals.append(jnp.sum(total[n] + start * back[n], axis=0, keepdims=True))
    ends = jnp.concatenate(ends, axis=0)
    adjoints = jnp.concatenate(adjoints, axis=0)
    lags = [jnp.sum(x, axis=0, keepdims=True) for x in lags]
    direct = lags[0]
    within = jnp.broadcast_to(lags[SUB - 1], (MODES, LANES))
    for d in reversed(range(SUB - 1)):
        within = row_ref[0] * within + lags[d]
    totals = row_ref[0] * jnp.concatenate(totals, axis=0) + within
    adjoints = adjoints + pltpu.roll(adjoints, HALF, 1)
    totals = totals + pltpu.roll(totals, HALF, 1)
    direct = direct + pltpu.roll(direct, HALF, 1)
    lanes_up = iota((MODES, LANES), 1) >= HALF
    write_message(
        msg_ref, jnp.where(lanes_up, ends, adjoints), packed_modes(totals), direct
    )


def local_outputs(
    pack_ref,
    mixed_ref, back_ref, after_ref, before_ref, block_ref, table_ref,
    steps_ref,
):
    rates = pack_ref[RATES : RATES + MODES]
    skip = pack_ref[SKIPS : SKIPS + SUB]
    wide = [lift(rates, m) for m in range(MODES)]
    factor = [jnp.exp(-r) for r in wide]
    weight = [lift(pack_ref, WEIGHTS + m) for m in range(MODES)]

    def run(source, dst_ref, start, flip):
        def body(i, state):
            step = STEPS - 1 - i if flip else i
            x = pack_ref[step_rows(source + step), :]
            state = [f * z + x for f, z in zip(factor, state)]
            dst_ref[step_rows(step), :] = (
                added([w * z for w, z in zip(weight, state)]) + skip * x
            )
            return state

        lax.fori_loop(0, STEPS, body, start, unroll=8)

    row = iota((SUB, LANES), 0)
    upper = iota((SUB, LANES), 1) >= HALF
    run(
        UNITS, steps_ref,
        [pack_ref[FORWARD + m * SUB : FORWARD + (m + 1) * SUB] for m in range(MODES)], False,
    )
    from_steps(steps_ref, mixed_ref)
    start_b = []
    for m in range(MODES):
        scan = pack_ref[BACKWARD + m * SUB : BACKWARD + (m + 1) * SUB]
        for d in (1, 2, 4):
            decay = jnp.where(row < SUB - d, jnp.exp(-float(STEPS * d) * wide[m]), 0.0)
            scan = scan + decay * pltpu.roll(scan, SUB - d, 0)
        first_other = pltpu.roll(lift(scan, 0), HALF, 1)
        start = jnp.where(row < SUB - 1, pltpu.roll(scan, SUB - 1, 0), 0.0)
        decay = jnp.exp(-(STEPS * (SUB - 1 - row).astype(F32)) * wide[m])
        start_b.append(start + jnp.where(upper, 0.0, decay * first_other))
    run(SIGNAL, steps_ref, start_b, True)
    from_steps(steps_ref, back_ref)

    rate_cols = turned_rows(rates)
    weight_cols = turned_rows(pack_ref[WEIGHTS : WEIGHTS + MODES])
    token = iota((HALF, LANES), 1).astype(F32)
    for m in range(MODES):
        r = jnp.broadcast_to(rate_cols[:HALF, m : m + 1], (HALF, LANES))
        w = jnp.broadcast_to(weight_cols[:HALF, m : m + 1], (HALF, LANES))
        after_ref[m] = w * jnp.exp(-(token + 1.0) * r)
        before_ref[m] = w * jnp.exp(-(LANES - token) * r)
        block_ref[m] = jnp.exp(-float(LANES) * r)
    lanes_up = iota((MODES, LANES), 1) >= HALF
    place = lax.rem(lax.axis_index("ctx"), GROUP)
    ahead = jnp.where(lanes_up, place, GROUP - 1 - place).astype(F32)
    table_ref[0] = jnp.exp(-rates)
    table_ref[1] = jnp.exp(-float(LOCAL * GROUP) * rates)
    table_ref[2] = jnp.exp(-(LOCAL * ahead) * rates)
    table_ref[3] = pack_ref[GAINS : GAINS + MODES] * NORM


def combine(got_ref, order, factor, rho, place):
    lanes_up = iota((MODES, LANES), 1) >= HALF
    zero = jnp.zeros((MODES, LANES), F32)
    firsts = [order.index(k) * ROWS for k in range(GROUP)]
    pairs = [got_ref[f : f + MODES] for f in firsts]
    fwd, bwd = zero, zero
    enter_f, enter_b = zero, zero
    cross = zero
    sums = jnp.zeros((SUB, LANES), F32)
    direct = jnp.zeros((1, LANES), F32)
    for k in range(GROUP):
        enter_f = jnp.where(place == k, fwd, enter_f)
        cross = cross + fwd * pltpu.roll(pairs[k], HALF, 1)
        fwd = rho * fwd + pairs[k]
        sums = sums + got_ref[firsts[k] + SUMS : firsts[k] + DIRECT]
        direct = direct + got_ref[firsts[k] + DIRECT : firsts[k] + ROWS]
    for k in reversed(range(GROUP)):
        enter_b = jnp.where(place == k, bwd, enter_b)
        bwd = rho * bwd + pairs[k]
    entering = jnp.where(lanes_up, enter_f, enter_b)
    joint = jnp.where(lanes_up, fwd, bwd)
    cross = factor * cross
    cross = jnp.where(lanes_up, cross, pltpu.roll(cross, HALF, 1))
    return joint, sums + packed_modes(cross), direct, entering


def starts_early():
    return lax.div(lax.axis_index("ctx"), GROUP) < EARLY


def first_plane():
    return lax.div(lax.axis_index("ctx"), GROUP) == 0


def one_way(rows, unit_ref, block_ref, local_ref, enter, blocks, full_ref, half):
    parts = [unit_ref[m, rows, :] * enter[:, m : m + 1] for m in range(MODES)]
    for n, b in enumerate(blocks):
        cols = slice(b * LANES, (b + 1) * LANES)
        full_ref[half * SUB : (half + 1) * SUB, cols] = local_ref[rows, cols] + added(parts)
        if n < len(blocks) - 1:
            parts = [x * block_ref[m, rows, :] for m, x in enumerate(parts)]


def halves(i):
    for half in range(2):
        yield half, pl.multiple_of(i * TALL + half * SUB, SUB)


def add_forward(i, enter_cols, mixed_ref, after_ref, block_ref, g_ref, gq_ref, full_ref):
    for half, first in halves(i):
        rows = pl.ds(first, SUB)
        enter = enter_cols[pl.ds(HALF + first, SUB), :]
        one_way(rows, after_ref, block_ref, mixed_ref, enter, range(8), full_ref, half)
    rows = pl.ds(pl.multiple_of(i * TALL, TALL), TALL)
    for b in range(8):
        cols = slice(b * LANES, (b + 1) * LANES)
        mixed = full_ref[:, cols]
        gq_ref[rows, cols] = (g_ref[rows, cols].astype(F32) * mixed).astype(jnp.bfloat16)


def add_backward(
    i, enter_cols, back_ref, before_ref, block_ref, k_ref, v_ref, gk_ref, gv_ref, full_ref
):
    for half, first in halves(i):
        rows = pl.ds(first, SUB)
        enter = enter_cols[rows, :]
        one_way(rows, before_ref, block_ref, back_ref, enter, range(7, -1, -1), full_ref, half)
    rows = pl.ds(pl.multiple_of(i * TALL, TALL), TALL)
    for b in range(8):
        cols = slice(b * LANES, (b + 1) * LANES)
        back = full_ref[:, cols]
        gk_ref[rows, cols] = (v_ref[rows, cols].astype(F32) * back).astype(jnp.bfloat16)
        gv_ref[rows, cols] = (k_ref[rows, cols].astype(F32) * back).astype(jnp.bfloat16)


def middle_kernel(got_ref, near_ref, pack_ref, g_ref, msg_ref, enter_ref, *refs):
    local, gq_ref, (steps_ref, enter_cols, full_ref) = refs[:6], refs[6], refs[7:]
    joint, sums, direct, entering = combine(
        got_ref, NEAR_ORDER, near_ref[0], near_ref[1], lax.rem(lax.axis_index("ctx"), GROUP)
    )
    enter_ref[...] = entering
    write_message(msg_ref, joint, sums, direct)

    @pl.when(starts_early())
    def _():
        local_outputs(pack_ref, *local, steps_ref)

    @pl.when(first_plane())
    def _():
        mixed_ref, _, after_ref, _, block_ref, _ = local
        enter_cols[...] = turned_rows(entering)

        def body(i, carry):
            add_forward(
                i, enter_cols, mixed_ref, after_ref, block_ref, g_ref, gq_ref, full_ref
            )
            return carry

        lax.fori_loop(0, HALF // TALL, body, 0, unroll=2)


def final_kernel(*refs):
    got, enter, pack, *early = refs[:9]
    ready, rest, late, steps = refs[9], refs[10:-7], refs[-7:-1], refs[-1]

    @pl.when(first_plane())
    def _():
        finish(got, enter, *early, ready, *rest)

    @pl.when(jnp.logical_and(starts_early(), jnp.logical_not(first_plane())))
    def _():
        finish(got, enter, *early, None, *rest)

    @pl.when(jnp.logical_not(starts_early()))
    def _():
        local_outputs(pack, *late, steps)
        finish(got, enter, *late, None, *rest)


def finish(
    got_ref, enter_ref, mixed_ref, back_ref, after_ref, before_ref, block_ref, table_ref,
    ready_ref, k_ref, v_ref, g_ref,
    gq_any, gk_any, gv_any, gr_any, gs_any,
    gq_ref, gk_ref, gv_ref, gr_ref, gs_ref, enter_cols, full_ref, sems, out_sems,
):
    copies = []
    if ready_ref is not None:
        copies.append(pltpu.make_async_copy(ready_ref, gq_any, sems.at[2]))
        copies[0].start()
    joint, sums, direct, outer = combine(
        got_ref, FAR_ORDER, table_ref[0], table_ref[1], lax.div(lax.axis_index("ctx"), GROUP)
    )
    enter_cols[...] = turned_rows(enter_ref[...] + table_ref[2] * outer)
    def out_copies(i):
        rows = pl.ds(pl.multiple_of(i * TALL, TALL), TALL)
        pairs = ((gk_ref, gk_any), (gv_ref, gv_any))
        if ready_ref is None:
            pairs += ((gq_ref, gq_any),)
        return [
            pltpu.make_async_copy(a.at[rows, :], b.at[rows, :], out_sems.at[n, i])
            for n, (a, b) in enumerate(pairs)
        ]

    def body(i, carry):
        if ready_ref is None:
            add_forward(
                i, enter_cols, mixed_ref, after_ref, block_ref, g_ref, gq_ref, full_ref.at[0]
            )
        add_backward(
            i, enter_cols, back_ref, before_ref, block_ref,
            k_ref, v_ref, gk_ref, gv_ref, full_ref.at[1],
        )
        for copy in out_copies(i):
            copy.start()
        return carry

    groups = HALF // TALL
    lax.fori_loop(0, groups - 1, body, 0, unroll=groups - 1)
    scaled = sums * packed_modes(table_ref[3])
    gr_ref[0:SUB] = scaled[:, :HALF]
    gr_ref[SUB:MODES] = scaled[:, HALF:]
    gs_ref[...] = direct[:, :HALF] * NORM
    small = [
        pltpu.make_async_copy(gr_ref, gr_any, sems.at[0]),
        pltpu.make_async_copy(gs_ref, gs_any, sems.at[1]),
    ]
    for copy in small:
        copy.start()
    copies.extend(small)
    lax.fori_loop(groups - 1, groups, body, 0, unroll=True)
    for i in range(HALF // TALL):
        copies.extend(out_copies(i))
    for copy in copies:
        copy.wait()


VMEM = pl.BlockSpec(memory_space=pltpu.VMEM)
ANY = pl.BlockSpec(memory_space=pl.ANY)
PARAMS = pltpu.CompilerParams(vmem_limit_bytes=32 * 1024 * 1024)
MESSAGE = jax.ShapeDtypeStruct((GROUP * ROWS, LANES), F32)


def exchange(msg, groups):
    rows = msg.reshape(GROUP * ROWS, 1, LANES)
    rows = lax.all_to_all(rows, "ctx", 0, 0, axis_index_groups=groups, tiled=True)
    return rows.reshape(GROUP * ROWS, LANES)


def shards(queries, keys, values, grad_out, residues, decay_rate, skip_gain):
    near = [[z * GROUP + k for k in NEAR_ORDER] for z in range(GROUP)]
    far = [[z * GROUP + k for z in FAR_ORDER] for k in range(GROUP)]
    wide = jax.ShapeDtypeStruct(queries.shape, jnp.bfloat16)
    held = pltpu.VMEM(queries.shape, jnp.bfloat16)

    stepped = pltpu.VMEM((PITCH * SUB + STEPS, LANES), F32)
    small = pltpu.VMEM((MODES, HALF), F32)
    packed = jax.ShapeDtypeStruct((PACK, LANES), F32)
    sources = (
        queries, keys, values, grad_out,
        decay_rate.T, residues.T, skip_gain.reshape(1, HALF),
    )
    pack, msg, near_table = pl.pallas_call(
        summary_kernel,
        out_shape=(packed, MESSAGE, jax.ShapeDtypeStruct((2, MODES, LANES), F32)),
        in_specs=[ANY] * 7,
        out_specs=(VMEM,) * 3,
        scratch_shapes=[held] * 4
        + [small, small, pltpu.VMEM((1, HALF), F32)]
        + [pltpu.VMEM((2 + STEPS // SUB, MODES, LANES), F32)]
        + [pltpu.VMEM((MODES, 5, SUB, LANES), F32), pltpu.SemaphoreType.DMA((3 + 4 * PARTS,))],
        compiler_params=PARAMS,
        name="summary",
    )(*(pltpu.with_memory_space_constraint(x, pltpu.HBM) for x in sources))
    got = exchange(msg, near)
    natural = jax.ShapeDtypeStruct(queries.shape, F32)
    units = jax.ShapeDtypeStruct((MODES, HALF, LANES), F32)
    local = (natural, natural, units, units, units)
    local = local + (jax.ShapeDtypeStruct((4, MODES, LANES), F32),)
    msg, enter, *early, ready = pl.pallas_call(
        middle_kernel,
        out_shape=(MESSAGE, jax.ShapeDtypeStruct((MODES, LANES), F32)) + local + (wide,),
        in_specs=[VMEM] * 4,
        out_specs=(VMEM,) * 9,
        scratch_shapes=[stepped, pltpu.VMEM((LANES, LANES), F32)]
        + [pltpu.VMEM((TALL, queries.shape[1]), F32)],
        compiler_params=PARAMS,
        name="middle",
    )(got, near_table, pack, grad_out)
    got = exchange(msg, far)
    grad_q, grad_k, grad_v, grad_res, grad_skip = pl.pallas_call(
        final_kernel,
        out_shape=(
            wide,
            wide,
            wide,
            jax.ShapeDtypeStruct((MODES, HALF), F32),
            jax.ShapeDtypeStruct((1, HALF), F32),
        ),
        in_specs=[VMEM] * 13,
        out_specs=(ANY,) * 5,
        scratch_shapes=[held] * 3
        + [small, pltpu.VMEM((1, HALF), F32), pltpu.VMEM((LANES, LANES), F32)]
        + [pltpu.VMEM((2, TALL, queries.shape[1]), F32)]
        + [pltpu.SemaphoreType.DMA((3,)), pltpu.SemaphoreType.DMA((3, HALF // TALL))]
        + [pltpu.VMEM(x.shape, F32) for x in local]
        + [stepped],
        compiler_params=PARAMS,
        name="final",
    )(got, enter, pack, *early, ready, keys, values, grad_out)
    return (grad_q, grad_k, grad_v, grad_res.T, grad_skip.reshape(HALF))


def solution(mesh):
    in_specs = (
        P("tp", "ctx"),
        P("tp", "ctx"),
        P("tp", "ctx"),
        P("tp", "ctx"),
        P("tp", None),
        P("tp", None),
        P("tp"),
    )
    out_specs = (P("tp", "ctx"), P("tp", "ctx"), P("tp", "ctx"), P("tp", None), P("tp"))
    return jax.shard_map(shards, mesh=mesh, in_specs=in_specs, out_specs=out_specs, check_vma=False)
```
